32 devices in a mesh: groups: 2 (over x), samp: 16 (over z, y, core).
Axes of the slice: x: 2, y: 2, z: 4, core: 2. Of those that a mesh axis runs over, the one named last changes fastest.
Arguments:
- queries: bfloat16 [16384, 4096], P(('groups', 'samp')), parts along dimension 0, may hold values from -40 to 40
- gen_panel: bfloat16 [512, 4096], P(('groups', 'samp')), parts along dimension 0, may hold values from -40 to 40
- ref_panel: bfloat16 [512, 4096], P(('groups', 'samp')), parts along dimension 0, may hold values from -40 to 40
Outputs:
- proof: float32 [16384], P(('groups', 'samp')), parts along dimension 0
The draws below stay inside these ranges and needn't reach their ends.
There are 2 independent parts, one for each index of `groups`. The reference program is written for one: setup_inputs(seed, part) draws one part's arguments, and reference() takes and returns one part's arrays. A program takes and returns all parts, laid end to end along the dimension named above; each array names one. Nothing has to cross between parts.
All inputs are finite; a program needn't handle non-finite values.
Results may differ from the reference program's by a relative error of at most 0.0003.
The reference program's roundings to bfloat16 on the way count: a program that leaves them out, or rounds other values in their place, can miss the bound.
Values may be sent and summed in bfloat16 or wider, within the bound.
No kernel may reach another device: no remote copies, remote signals or barrier semaphores. Data moves between devices by JAX's collectives and lax.ppermute only.
A program may use at most 64 MiB of HBM per device.

```python
import jax
import jax.numpy as jnp

F = 4096
TEMP = 64
EVAL_ROWS = 8192
PANEL_ROWS = 256


def shared_profile(key):
    return 15.0 * jnp.clip(jax.random.normal(jax.random.fold_in(key, 99), (F,), jnp.float32), -2.0, 2.0)


def scaled_rows(key, noise, low, high, profile):
    count = noise.shape[0]
    scales = jnp.exp(jax.random.uniform(key, (count, 1), jnp.float32, jnp.log(low), jnp.log(high)))
    return (profile + scales * noise).astype(jnp.bfloat16)


def normal_noise(key, count):
    return jnp.clip(jax.random.normal(key, (count, F), jnp.float32), -6.0, 6.0)


def draw_queries(key, part):
    profile = shared_profile(key)
    key = jax.random.fold_in(key, 1)
    key_scale, key_noise = jax.random.split(key)
    return scaled_rows(key_scale, normal_noise(key_noise, EVAL_ROWS), 0.7, 1.4, profile)


def draw_gen_panel(key, part):
    profile = shared_profile(key)
    key = jax.random.fold_in(key, 2)
    key_scale, key_noise = jax.random.split(key)
    return scaled_rows(key_scale, normal_noise(key_noise, PANEL_ROWS), 0.99, 1.01, profile)


def draw_ref_panel(key, part):
    profile = shared_profile(key)
    key = jax.random.fold_in(key, 3)
    key_scale, key_noise = jax.random.split(key)
    return scaled_rows(key_scale, normal_noise(key_noise, PANEL_ROWS), 0.99, 1.01, profile)


def setup_inputs(seed: int = 0, part: int = 0) -> dict:
    arg_keys = jax.random.split(jax.random.key(seed), 4)
    part_splits = jax.random.split(jax.random.fold_in(arg_keys[3], part), 4)
    queries = draw_queries(jax.random.fold_in(jax.random.fold_in(arg_keys[3], part), 71), part)
    gen_panel = draw_gen_panel(jax.random.fold_in(jax.random.fold_in(arg_keys[3], part), 71), part)
    ref_panel = draw_ref_panel(jax.random.fold_in(jax.random.fold_in(arg_keys[3], part), 71), part)
    return {"queries": queries, "gen_panel": gen_panel, "ref_panel": ref_panel}


def center_rows(rows, profile):
    return (rows.astype(jnp.float32) - profile).astype(jnp.bfloat16)


def reference(queries, gen_panel, ref_panel):
    profile = jnp.sum(ref_panel.astype(jnp.float32), axis=0) / ref_panel.shape[0]
    probes = center_rows(queries, profile)

    def log_sum(panel):
        centered = center_rows(panel, profile)
        half_norm = 0.5 * jnp.sum(jnp.square(centered.astype(jnp.float32)), axis=1)
        scores = (jnp.dot(probes, centered.T, preferred_element_type=jnp.float32) - half_norm) / TEMP
        return jax.nn.logsumexp(scores, axis=1)

    return log_sum(gen_panel) - log_sum(ref_panel)
```

```python
import jax
import jax.numpy as jnp
from jax import lax
from jax.sharding import PartitionSpec as P

TEMP = 64


def center_rows(rows, profile):
    centered = rows.astype(jnp.float32) - profile
    return lax.reduce_precision(centered, 8, 7).astype(jnp.bfloat16)


def half_norms(centered):
    return 0.5 * jnp.sum(jnp.square(centered.astype(jnp.float32)), axis=1)


def panel_scores(probes, panel):
    products = lax.dot_general(
        probes, panel, (((1,), (1,)), ((), ())), preferred_element_type=jnp.float32
    )
    return (products - half_norms(panel)) / TEMP


def body(queries, gen_panel, ref_panel):
    both = jnp.stack([ref_panel, gen_panel])
    every = lax.all_gather(both, "samp", axis=1, tiled=True)
    ref_all, gen_all = every[0], every[1]
    profile = jnp.sum(ref_all.astype(jnp.float32), axis=0) / ref_all.shape[0]
    probes = center_rows(queries, profile)
    gen_c = center_rows(gen_all, profile)
    ref_c = center_rows(ref_all, profile)
    gen_log = jax.nn.logsumexp(panel_scores(probes, gen_c), axis=1)
    ref_log = jax.nn.logsumexp(panel_scores(probes, ref_c), axis=1)
    return gen_log - ref_log


def solution(mesh):
    return jax.shard_map(
        body,
        mesh=mesh,
        in_specs=(
            P(("groups", "samp"), None),
            P(("groups", "samp"), None),
            P(("groups", "samp"), None),
        ),
        out_specs=P(("groups", "samp")),
        check_vma=False,
    )
```

```python
import jax
import jax.numpy as jnp
from jax import lax
from jax.sharding import PartitionSpec as P

TEMP = 64


def ring_of_chips(chips):
    return list(range(0, chips, 2)) + list(range(chips - 1 - chips % 2, 0, -2))


def ring_pairs(size):
    order = ring_of_chips(size // 2)
    pairs = []
    for place, chip in enumerate(order):
        after = order[(place + 1) % len(order)]
        before = order[place - 1]
        pairs.append((2 * chip, 2 * after))
        pairs.append((2 * chip + 1, 2 * before + 1))
    return pairs


def core_pairs(size):
    return [(i, i ^ 1) for i in range(size)]


def gather_pieces(own, size):
    twins, ring = core_pairs(size), ring_pairs(size)
    chips = size // 2
    core = lax.axis_index("samp") % 2
    other = lax.ppermute(own, "samp", twins)
    block = jnp.concatenate([own, other], axis=1)
    pieces = [block]
    steps = (chips - 1) // 2
    for _ in range(steps):
        block = lax.ppermute(block, "samp", ring)
        pieces += [block, lax.ppermute(block, "samp", twins)]
    if chips % 2 == 0:
        half = block.shape[1] // 2
        last = lax.ppermute(block[:, :half], "samp", ring)
        pieces += [last, lax.ppermute(last, "samp", twins)]
    return pieces


def center_rows(rows, profile):
    centered = rows.astype(jnp.float32) - profile
    return lax.reduce_precision(centered, 8, 7).astype(jnp.bfloat16)


def half_norms(centered):
    return 0.5 * jnp.sum(jnp.square(centered.astype(jnp.float32)), axis=1)


def panel_scores(probes, panel):
    products = lax.dot_general(
        probes, panel, (((1,), (1,)), ((), ())), preferred_element_type=jnp.float32
    )
    return (products - half_norms(panel)) / TEMP


def body(queries, gen_panel, ref_panel):
    size = lax.axis_size("samp")
    pieces = gather_pieces(jnp.stack([ref_panel, gen_panel]), size)
    every = jnp.concatenate(pieces, axis=1)
    ref_all, gen_all = every[0], every[1]
    profile = jnp.sum(ref_all.astype(jnp.float32), axis=0) / ref_all.shape[0]
    probes = center_rows(queries, profile)
    gen_c = center_rows(gen_all, profile)
    ref_c = center_rows(ref_all, profile)
    gen_log = jax.nn.logsumexp(panel_scores(probes, gen_c), axis=1)
    ref_log = jax.nn.logsumexp(panel_scores(probes, ref_c), axis=1)
    return gen_log - ref_log


def solution(mesh):
    return jax.shard_map(
        body,
        mesh=mesh,
        in_specs=(
            P(("groups", "samp"), None),
            P(("groups", "samp"), None),
            P(("groups", "samp"), None),
        ),
        out_specs=P(("groups", "samp")),
        check_vma=False,
    )
```

```python
import jax
import jax.numpy as jnp
from jax import lax
from jax.sharding import PartitionSpec as P

TEMP = 64


def ring_of_chips(chips):
    return list(range(0, chips, 2)) + list(range(chips - 1 - chips % 2, 0, -2))


def ring_pairs(size):
    order = ring_of_chips(size // 2)
    pairs = []
    for place, chip in enumerate(order):
        after = order[(place + 1) % len(order)]
        before = order[place - 1]
        pairs.append((2 * chip, 2 * after))
        pairs.append((2 * chip + 1, 2 * before + 1))
    return pairs


def core_pairs(size):
    return [(i, i ^ 1) for i in range(size)]


def gather_pieces(own, size):
    twins, ring = core_pairs(size), ring_pairs(size)
    chips = size // 2

    def hop(block):
        return lax.ppermute(block, "samp", ring)

    def hand_over(block):
        return lax.ppermute(block, "samp", twins)

    steps = (chips - 1) // 2
    mine = own
    pieces = [own]
    other = hand_over(own)
    pieces.append(other)
    for _ in range(steps):
        mine, other = hop(mine), hop(other)
        pieces += [mine, other, hand_over(mine), hand_over(other)]
    if chips % 2 == 0:
        mine = hop(mine)
        pieces += [mine, hand_over(mine)]
    return pieces


def center_rows(rows, profile):
    centered = rows.astype(jnp.float32) - profile
    return lax.reduce_precision(centered, 8, 7).astype(jnp.bfloat16)


def half_norms(centered):
    return 0.5 * jnp.sum(jnp.square(centered.astype(jnp.float32)), axis=1)


def panel_scores(probes, panel):
    products = lax.dot_general(
        probes, panel, (((1,), (1,)), ((), ())), preferred_element_type=jnp.float32
    )
    return (products - half_norms(panel)) / TEMP


def body(queries, gen_panel, ref_panel):
    size = lax.axis_size("samp")
    pieces = gather_pieces(jnp.stack([ref_panel, gen_panel]), size)
    every = jnp.concatenate(pieces, axis=1)
    ref_all, gen_all = every[0], every[1]
    profile = jnp.sum(ref_all.astype(jnp.float32), axis=0) / ref_all.shape[0]
    probes = center_rows(queries, profile)
    gen_c = center_rows(gen_all, profile)
    ref_c = center_rows(ref_all, profile)
    gen_log = jax.nn.logsumexp(panel_scores(probes, gen_c), axis=1)
    ref_log = jax.nn.logsumexp(panel_scores(probes, ref_c), axis=1)
    return gen_log - ref_log


def solution(mesh):
    return jax.shard_map(
        body,
        mesh=mesh,
        in_specs=(
            P(("groups", "samp"), None),
            P(("groups", "samp"), None),
            P(("groups", "samp"), None),
        ),
        out_specs=P(("groups", "samp")),
        check_vma=False,
    )
```

```python
import jax
import jax.numpy as jnp
from jax import lax
from jax.sharding import PartitionSpec as P

TEMP = 64


def ring_of_chips(chips):
    return list(range(0, chips, 2)) + list(range(chips - 1 - chips % 2, 0, -2))


def ring_pairs(size):
    order = ring_of_chips(size // 2)
    pairs = []
    for place, chip in enumerate(order):
        after = order[(place + 1) % len(order)]
        before = order[place - 1]
        pairs.append((2 * chip, 2 * after))
        pairs.append((2 * chip + 1, 2 * before + 1))
    return pairs


def core_pairs(size):
    return [(i, i ^ 1) for i in range(size)]


def gather_pieces(block, size):
    twins, ring = core_pairs(size), ring_pairs(size)
    chips = size // 2
    pieces = [block]
    for _ in range((chips - 1) // 2):
        block = lax.ppermute(block, "samp", ring)
        pieces += [block, lax.ppermute(block, "samp", twins)]
    if chips % 2 == 0:
        block = lax.ppermute(block[: block.shape[0] // 2], "samp", ring)
        pieces += [block, lax.ppermute(block, "samp", twins)]
    return pieces


def center_rows(rows, profile):
    centered = rows.astype(jnp.float32) - profile
    return lax.reduce_precision(centered, 8, 7).astype(jnp.bfloat16)


def half_norms(centered):
    return 0.5 * jnp.sum(jnp.square(centered.astype(jnp.float32)), axis=1)


def panel_scores(probes, panel):
    products = lax.dot_general(
        probes, panel, (((1,), (1,)), ((), ())), preferred_element_type=jnp.float32
    )
    return (products - half_norms(panel)) / TEMP


def body(queries, gen_panel, ref_panel):
    size = lax.axis_size("samp")
    own = lax.optimization_barrier(jnp.stack([ref_panel, gen_panel]))
    other = lax.ppermute(own, "samp", core_pairs(size))
    chip = jnp.concatenate([own, other], axis=1)
    ref_all = jnp.concatenate(gather_pieces(chip[0], size), axis=0)
    gen_all = jnp.concatenate(gather_pieces(chip[1], size), axis=0)
    profile = jnp.sum(ref_all.astype(jnp.float32), axis=0) / ref_all.shape[0]
    probes = center_rows(queries, profile)
    gen_c = center_rows(gen_all, profile)
    ref_c = center_rows(ref_all, profile)
    gen_log = jax.nn.logsumexp(panel_scores(probes, gen_c), axis=1)
    ref_log = jax.nn.logsumexp(panel_scores(probes, ref_c), axis=1)
    return gen_log - ref_log


def solution(mesh):
    return jax.shard_map(
        body,
        mesh=mesh,
        in_specs=(
            P(("groups", "samp"), None),
            P(("groups", "samp"), None),
            P(("groups", "samp"), None),
        ),
        out_specs=P(("groups", "samp")),
        check_vma=False,
    )
```

```python
import jax
import jax.numpy as jnp
from jax import lax
from jax.experimental import pallas as pl
from jax.experimental.pallas import tpu as pltpu
from jax.sharding import PartitionSpec as P

TEMP = 64
LANES = 128
CHUNK = 1024
GROUP = 32
LIMIT = 40 * 2**20


def ring_of_chips(chips):
    return list(range(0, chips, 2)) + list(range(chips - 1 - chips % 2, 0, -2))


def ring_pairs(size):
    order = ring_of_chips(size // 2)
    pairs = []
    for place, chip in enumerate(order):
        after = order[(place + 1) % len(order)]
        before = order[place - 1]
        pairs.append((2 * chip, 2 * after))
        pairs.append((2 * chip + 1, 2 * before + 1))
    return pairs


def core_pairs(size):
    return [(i, i ^ 1) for i in range(size)]


def gather_pieces(block, size):
    twins, ring = core_pairs(size), ring_pairs(size)
    chips = size // 2
    pieces = [block]
    for _ in range((chips - 1) // 2):
        block = lax.ppermute(block, "samp", ring)
        pieces += [block, lax.ppermute(block, "samp", twins)]
    if chips % 2 == 0:
        block = lax.ppermute(block[: block.shape[0] // 2], "samp", ring)
        pieces += [block, lax.ppermute(block, "samp", twins)]
    return pieces


def row_groups(rows, step):
    return [slice(r, min(r + step, rows)) for r in range(0, rows, step)]


def center(rows, mean):
    return (rows.astype(jnp.float32) - mean).astype(jnp.bfloat16)


def add_panel_chunk(cols, mean, panel, probes, centered, squares, scores, first):
    for rows in row_groups(panel.shape[0], GROUP):
        part = center(panel[rows, cols], mean)
        centered[rows, cols] = part
        wide = jnp.square(part.astype(jnp.float32))
        total = wide[:, :LANES]
        for lane in range(LANES, wide.shape[1], LANES):
            total += wide[:, lane : lane + LANES]
        squares[rows, :] = total if first else squares[rows, :] + total
    products = lax.dot_general(
        centered[:, cols], probes[:, cols], (((1,), (1,)), ((), ())),
        preferred_element_type=jnp.float32,
    )
    scores[...] = products if first else scores[...] + products


def log_sum(squares, scores):
    half = 0.5 * jnp.sum(squares[...], axis=1, keepdims=True)
    x = (scores[...] - half) / TEMP
    top = jnp.max(x, axis=0, keepdims=True)
    return jnp.log(jnp.sum(jnp.exp(x - top), axis=0, keepdims=True)) + top


def ref_kernel(queries, panel, probes, mean, ref_log, centered, squares, scores):
    count, features = panel.shape
    for start in range(0, features, CHUNK):
        cols = slice(start, start + CHUNK)
        total = None
        for rows in row_groups(count, GROUP):
            part = jnp.sum(panel[rows, cols].astype(jnp.float32), axis=0, keepdims=True)
            total = part if total is None else total + part
        here = total / count
        mean[:, cols] = here
        for rows in row_groups(queries.shape[0], GROUP):
            probes[rows, cols] = center(queries[rows, cols], here)
        add_panel_chunk(cols, here, panel, probes, centered, squares, scores, start == 0)
    ref_log[...] = log_sum(squares, scores)


def gen_kernel(probes, mean, panel, ref_log, proof, centered, squares, scores):
    for start in range(0, panel.shape[1], CHUNK):
        cols = slice(start, start + CHUNK)
        add_panel_chunk(cols, mean[:, cols], panel, probes, centered, squares, scores, start == 0)
    proof[...] = log_sum(squares, scores) - ref_log[...]


def scratch(panel, queries):
    count, features = panel.shape
    return [
        pltpu.VMEM((count, features), jnp.bfloat16),
        pltpu.VMEM((count, LANES), jnp.float32),
        pltpu.VMEM((count, queries.shape[0]), jnp.float32),
    ]


def in_vmem(n):
    return [pl.BlockSpec(memory_space=pltpu.VMEM)] * n


def cost(queries, panel):
    work = queries.shape[0] * panel.shape[0]
    return pl.CostEstimate(
        flops=2 * work * panel.shape[1],
        bytes_accessed=2 * (queries.size + panel.size),
        transcendentals=work,
    )


def score_ref(queries, panel):
    count, features = queries.shape
    return pl.pallas_call(
        ref_kernel,
        out_shape=(
            jax.ShapeDtypeStruct((count, features), jnp.bfloat16),
            jax.ShapeDtypeStruct((1, features), jnp.float32),
            jax.ShapeDtypeStruct((1, count), jnp.float32),
        ),
        in_specs=in_vmem(2),
        out_specs=tuple(in_vmem(3)),
        scratch_shapes=scratch(panel, queries),
        compiler_params=pltpu.CompilerParams(vmem_limit_bytes=LIMIT),
        cost_estimate=cost(queries, panel),
    )(queries, panel)


def score_gen(probes, mean, panel, ref_log):
    return pl.pallas_call(
        gen_kernel,
        out_shape=jax.ShapeDtypeStruct((1, probes.shape[0]), jnp.float32),
        in_specs=in_vmem(4),
        out_specs=in_vmem(1)[0],
        scratch_shapes=scratch(panel, probes),
        compiler_params=pltpu.CompilerParams(vmem_limit_bytes=LIMIT),
        cost_estimate=cost(probes, panel),
    )(probes, mean, panel, ref_log)


def body(queries, gen_panel, ref_panel):
    size = lax.axis_size("samp")
    own = lax.optimization_barrier(jnp.stack([ref_panel, gen_panel]))
    other = lax.ppermute(own, "samp", core_pairs(size))
    chip = jnp.concatenate([own, other], axis=1)
    ref_all = jnp.concatenate(gather_pieces(chip[0], size), axis=0)
    gen_all = jnp.concatenate(gather_pieces(chip[1], size), axis=0)
    probes, mean, ref_log = score_ref(queries, ref_all)
    return score_gen(probes, mean, gen_all, ref_log).reshape(-1)


def solution(mesh):
    return jax.shard_map(
        body,
        mesh=mesh,
        in_specs=(
            P(("groups", "samp"), None),
            P(("groups", "samp"), None),
            P(("groups", "samp"), None),
        ),
        out_specs=P(("groups", "samp")),
        check_vma=False,
    )
```

```python
import jax
import jax.numpy as jnp
from jax import lax
from jax.experimental import pallas as pl
from jax.experimental.pallas import tpu as pltpu
from jax.sharding import PartitionSpec as P

TEMP = 64
LANES = 128
CHUNK = 1024
GROUP = 32
LIMIT = 40 * 2**20


def ring_of_chips(chips):
    return list(range(0, chips, 2)) + list(range(chips - 1 - chips % 2, 0, -2))


def ring_pairs(size):
    order = ring_of_chips(size // 2)
    pairs = []
    for place, chip in enumerate(order):
        after = order[(place + 1) % len(order)]
        before = order[place - 1]
        pairs.append((2 * chip, 2 * after))
        pairs.append((2 * chip + 1, 2 * before + 1))
    return pairs


def core_pairs(size):
    return [(i, i ^ 1) for i in range(size)]


def gather_panels(panels, size):
    twins, ring = core_pairs(size), ring_pairs(size)
    chips = size // 2

    def hop(block):
        return lax.ppermute(block, "samp", ring)

    def hand_over(block):
        return lax.ppermute(block, "samp", twins)

    mine = list(panels)
    other = [hand_over(p) for p in mine]
    pieces = [[m, o] for m, o in zip(mine, other)]
    for _ in range((chips - 1) // 2):
        for i in range(len(panels)):
            mine[i], other[i] = hop(mine[i]), hop(other[i])
            both = jnp.concatenate([mine[i], other[i]], axis=0)
            pieces[i] += [both, hand_over(both)]
    if chips % 2 == 0:
        for i in range(len(panels)):
            mine[i] = hop(mine[i])
            pieces[i] += [mine[i], hand_over(mine[i])]
    return [jnp.concatenate(p, axis=0) for p in pieces]


def row_groups(rows, step):
    return [slice(r, min(r + step, rows)) for r in range(0, rows, step)]


def center(rows, mean):
    return (rows.astype(jnp.float32) - mean).astype(jnp.bfloat16)


def add_panel_chunk(cols, mean, panel, probes, centered, squares, scores, first):
    for rows in row_groups(panel.shape[0], GROUP):
        part = center(panel[rows, cols], mean)
        centered[rows, cols] = part
        wide = jnp.square(part.astype(jnp.float32))
        total = wide[:, :LANES]
        for lane in range(LANES, wide.shape[1], LANES):
            total += wide[:, lane : lane + LANES]
        squares[rows, :] = total if first else squares[rows, :] + total
    products = lax.dot_general(
        centered[:, cols], probes[:, cols], (((1,), (1,)), ((), ())),
        preferred_element_type=jnp.float32,
    )
    scores[...] = products if first else scores[...] + products


def log_sum(squares, scores):
    half = 0.5 * jnp.sum(squares[...], axis=1, keepdims=True)
    x = (scores[...] - half) / TEMP
    top = jnp.max(x, axis=0, keepdims=True)
    return jnp.log(jnp.sum(jnp.exp(x - top), axis=0, keepdims=True)) + top


def ref_kernel(queries, panel, probes, mean, ref_log, centered, squares, scores):
    count, features = panel.shape
    for start in range(0, features, CHUNK):
        cols = slice(start, start + CHUNK)
        total = None
        for rows in row_groups(count, GROUP):
            part = jnp.sum(panel[rows, cols].astype(jnp.float32), axis=0, keepdims=True)
            total = part if total is None else total + part
        here = total / count
        mean[:, cols] = here
        for rows in row_groups(queries.shape[0], GROUP):
            probes[rows, cols] = center(queries[rows, cols], here)
        add_panel_chunk(cols, here, panel, probes, centered, squares, scores, start == 0)
    ref_log[...] = log_sum(squares, scores)


def gen_kernel(probes, mean, panel, ref_log, proof, centered, squares, scores):
    for start in range(0, panel.shape[1], CHUNK):
        cols = slice(start, start + CHUNK)
        add_panel_chunk(cols, mean[:, cols], panel, probes, centered, squares, scores, start == 0)
    proof[...] = log_sum(squares, scores) - ref_log[...]


def scratch(panel, queries):
    count, features = panel.shape
    return [
        pltpu.VMEM((count, features), jnp.bfloat16),
        pltpu.VMEM((count, LANES), jnp.float32),
        pltpu.VMEM((count, queries.shape[0]), jnp.float32),
    ]


def in_vmem(n):
    return [pl.BlockSpec(memory_space=pltpu.VMEM)] * n


def cost(queries, panel):
    work = queries.shape[0] * panel.shape[0]
    return pl.CostEstimate(
        flops=2 * work * panel.shape[1],
        bytes_accessed=2 * (queries.size + panel.size),
        transcendentals=work,
    )


def score_ref(queries, panel):
    count, features = queries.shape
    return pl.pallas_call(
        ref_kernel,
        out_shape=(
            jax.ShapeDtypeStruct((count, features), jnp.bfloat16),
            jax.ShapeDtypeStruct((1, features), jnp.float32),
            jax.ShapeDtypeStruct((1, count), jnp.float32),
        ),
        in_specs=in_vmem(2),
        out_specs=tuple(in_vmem(3)),
        scratch_shapes=scratch(panel, queries),
        compiler_params=pltpu.CompilerParams(vmem_limit_bytes=LIMIT),
        cost_estimate=cost(queries, panel),
    )(queries, panel)


def score_gen(probes, mean, panel, ref_log):
    return pl.pallas_call(
        gen_kernel,
        out_shape=jax.ShapeDtypeStruct((1, probes.shape[0]), jnp.float32),
        in_specs=in_vmem(4),
        out_specs=in_vmem(1)[0],
        scratch_shapes=scratch(panel, probes),
        compiler_params=pltpu.CompilerParams(vmem_limit_bytes=LIMIT),
        cost_estimate=cost(probes, panel),
    )(probes, mean, panel, ref_log)


def body(queries, gen_panel, ref_panel):
    size = lax.axis_size("samp")
    gen_all, ref_all = gather_panels([gen_panel, ref_panel], size)
    probes, mean, ref_log = score_ref(queries, ref_all)
    return score_gen(probes, mean, gen_all, ref_log).reshape(-1)


def solution(mesh):
    return jax.shard_map(
        body,
        mesh=mesh,
        in_specs=(
            P(("groups", "samp"), None),
            P(("groups", "samp"), None),
            P(("groups", "samp"), None),
        ),
        out_specs=P(("groups", "samp")),
        check_vma=False,
    )
```

```python
import jax
import jax.numpy as jnp
from jax import lax
from jax.experimental import pallas as pl
from jax.experimental.pallas import tpu as pltpu
from jax.sharding import PartitionSpec as P

TEMP = 64
LANES = 128
CHUNK = 1024
GROUP = 32
LIMIT = 40 * 2**20


def ring_of_chips(chips):
    return list(range(0, chips, 2)) + list(range(chips - 1 - chips % 2, 0, -2))


def ring_pairs(size, way):
    order = ring_of_chips(size // 2)
    pairs = []
    for place, chip in enumerate(order):
        to = order[(place + way) % len(order)]
        pairs += [(2 * chip + core, 2 * to + core) for core in range(2)]
    return pairs


def gather_panels(panels, size):
    chips, rows = size // 2, panels[0].shape[0]
    to_twin = [(i, i ^ 1) for i in range(size)]
    ways = [ring_pairs(size, 1), ring_pairs(size, -1)]

    def hop(block, way):
        return lax.ppermute(block, "samp", ways[way])

    def hand_over(block):
        return lax.ppermute(block, "samp", to_twin)

    chains = [list(panels), list(panels)]
    pieces = [[] for _ in panels]
    steps = (chips - 1) // 2
    if steps == 0:
        pieces = [[hand_over(p)] for p in panels]
    for step in range(steps):
        for i in range(len(panels)):
            for way in range(2):
                chains[way][i] = hop(chains[way][i], way)
        arrived = [[chains[way][i] for way in range(2)] for i in range(len(panels))]
        if step == 0:
            give = [[p] + a for p, a in zip(panels, arrived)]
        else:
            give = arrived
        given = hand_over(jnp.concatenate(give[0] + give[1], axis=0))
        count = rows * len(give[0])
        for i in range(len(panels)):
            pieces[i] += arrived[i] + [given[count * i : count * (i + 1)]]
    if chips % 2 == 0:
        for i in range(len(panels)):
            last = hop(chains[1 - i][i], 1 - i)
            pieces[i] += [last, hand_over(last)]
    return [jnp.concatenate(p, axis=0) for p in pieces]


def row_groups(rows, step):
    return [slice(r, min(r + step, rows)) for r in range(0, rows, step)]


def center(rows, mean):
    return (rows.astype(jnp.float32) - mean).astype(jnp.bfloat16)


def add_panel_chunk(cols, mean, panels, probes, centered, squares, scores, first):
    at = 0
    for panel in panels:
        for rows in row_groups(panel.shape[0], GROUP):
            here = slice(at, at + rows.stop - rows.start)
            at = here.stop
            part = center(panel[rows, cols], mean)
            centered[here, cols] = part
            wide = jnp.square(part.astype(jnp.float32))
            total = wide[:, :LANES]
            for lane in range(LANES, wide.shape[1], LANES):
                total += wide[:, lane : lane + LANES]
            squares[here, :] = total if first else squares[here, :] + total
    products = lax.dot_general(
        centered[:, cols], probes[:, cols], (((1,), (1,)), ((), ())),
        preferred_element_type=jnp.float32,
    )
    scores[...] = products if first else scores[...] + products


def log_sum(squares, scores):
    half = 0.5 * jnp.sum(squares[...], axis=1, keepdims=True)
    x = (scores[...] - half) / TEMP
    top = jnp.max(x, axis=0, keepdims=True)
    return jnp.log(jnp.sum(jnp.exp(x - top), axis=0, keepdims=True)) + top


def ref_kernel(queries, own, others, probes, mean, ref_log, centered, squares, scores):
    panels = (own, others)
    count, features = centered.shape
    for start in range(0, features, CHUNK):
        cols = slice(start, start + CHUNK)
        total = None
        for panel in panels:
            for rows in row_groups(panel.shape[0], GROUP):
                part = jnp.sum(panel[rows, cols].astype(jnp.float32), axis=0, keepdims=True)
                total = part if total is None else total + part
        here = total / count
        mean[:, cols] = here
        for rows in row_groups(queries.shape[0], GROUP):
            probes[rows, cols] = center(queries[rows, cols], here)
        add_panel_chunk(cols, here, panels, probes, centered, squares, scores, start == 0)
    ref_log[...] = log_sum(squares, scores)


def gen_kernel(probes, mean, own, others, ref_log, proof, centered, squares, scores):
    panels = (own, others)
    for start in range(0, centered.shape[1], CHUNK):
        cols = slice(start, start + CHUNK)
        add_panel_chunk(cols, mean[:, cols], panels, probes, centered, squares, scores, start == 0)
    proof[...] = log_sum(squares, scores) - ref_log[...]


def in_vmem(n):
    return [pl.BlockSpec(memory_space=pltpu.VMEM)] * n


def call_options(queries, own, others):
    rows, (count, features) = own.shape[0] + others.shape[0], queries.shape
    return dict(
        scratch_shapes=[
            pltpu.VMEM((rows, features), jnp.bfloat16),
            pltpu.VMEM((rows, LANES), jnp.float32),
            pltpu.VMEM((rows, count), jnp.float32),
        ],
        compiler_params=pltpu.CompilerParams(vmem_limit_bytes=LIMIT),
        cost_estimate=pl.CostEstimate(
            flops=2 * rows * count * features,
            bytes_accessed=2 * (rows + count) * features,
            transcendentals=rows * count,
        ),
    )


def score_ref(queries, own, others):
    count, features = queries.shape
    return pl.pallas_call(
        ref_kernel,
        out_shape=(
            jax.ShapeDtypeStruct((count, features), jnp.bfloat16),
            jax.ShapeDtypeStruct((1, features), jnp.float32),
            jax.ShapeDtypeStruct((1, count), jnp.float32),
        ),
        in_specs=in_vmem(3),
        out_specs=tuple(in_vmem(3)),
        **call_options(queries, own, others),
    )(queries, own, others)


def score_gen(probes, mean, own, others, ref_log):
    return pl.pallas_call(
        gen_kernel,
        out_shape=jax.ShapeDtypeStruct((1, probes.shape[0]), jnp.float32),
        in_specs=in_vmem(5),
        out_specs=in_vmem(1)[0],
        **call_options(probes, own, others),
    )(probes, mean, own, others, ref_log)


def body(queries, gen_panel, ref_panel):
    size = lax.axis_size("samp")
    ref_others, gen_others = gather_panels([ref_panel, gen_panel], size)
    probes, mean, ref_log = score_ref(queries, ref_panel, ref_others)
    return score_gen(probes, mean, gen_panel, gen_others, ref_log).reshape(-1)


def solution(mesh):
    return jax.shard_map(
        body,
        mesh=mesh,
        in_specs=(
            P(("groups", "samp"), None),
            P(("groups", "samp"), None),
            P(("groups", "samp"), None),
        ),
        out_specs=P(("groups", "samp")),
        check_vma=False,
    )
```

```python
import functools

import jax
import jax.numpy as jnp
from jax import lax
from jax.experimental import pallas as pl
from jax.experimental.pallas import tpu as pltpu
from jax.sharding import PartitionSpec as P

TEMP = 64
LANES = 128
CHUNK = 1024
GROUP = 32
LIMIT = 40 * 2**20


def ring_of_chips(chips):
    return list(range(0, chips, 2)) + list(range(chips - 1 - chips % 2, 0, -2))


def ring_pairs(size):
    order = ring_of_chips(size // 2)
    pairs = []
    for place, chip in enumerate(order):
        after = order[(place + 1) % len(order)]
        before = order[place - 1]
        pairs.append((2 * chip, 2 * after))
        pairs.append((2 * chip + 1, 2 * before + 1))
    return pairs


def core_pairs(size):
    return [(i, i ^ 1) for i in range(size)]


def gather_panels(panels, early, size):
    twins, ring = core_pairs(size), ring_pairs(size)
    chips, rows = size // 2, panels[0].shape[0]

    def hop(block):
        return lax.ppermute(block, "samp", ring)

    def hand_over(block):
        return lax.ppermute(block, "samp", twins)

    steps = (chips - 1) // 2
    mine, other = list(panels), None
    pieces = [[(p, 0, rows)] for p in panels]
    fresh = [[] for _ in panels]
    for period in range(steps + 1):
        last = period == steps
        if period == 1:
            mine[0], early = lax.optimization_barrier((mine[0], early))
        other = [hop(o) for o in other] if period else [hand_over(p) for p in panels]
        arrived = [[] for _ in panels]
        if not last or chips % 2 == 0:
            mine = [hop(m) for m in mine]
            arrived = [[m] for m in mine]
        for i, o in enumerate(other):
            pieces[i] += [(a, 0, rows) for a in arrived[i] + [o]]
            fresh[i] += arrived[i] + ([o] if period else [])
        if last:
            for i in range(len(panels)):
                if fresh[i]:
                    block = hand_over(jnp.concatenate(fresh[i], axis=0))
                    pieces[i].append((block, 0, block.shape[0]))
        elif period:
            block, at = hand_over(jnp.concatenate([f for g in fresh for f in g], axis=0)), 0
            for i in range(len(panels)):
                upto = at + rows * len(fresh[i])
                pieces[i].append((block, at, upto))
                fresh[i], at = [], upto
    return pieces, early


def row_groups(rows, step):
    return [slice(r, min(r + step, rows)) for r in range(0, rows, step)]


def panel_groups(refs, spans):
    groups, at = [], 0
    for ref, (low, high) in zip(refs, spans):
        for rows in row_groups(high - low, GROUP):
            size = rows.stop - rows.start
            groups.append((ref, slice(low + rows.start, low + rows.stop), slice(at, at + size)))
            at += size
    return groups


def center(rows, mean):
    return (rows.astype(jnp.float32) - mean).astype(jnp.bfloat16)


def center_panel_chunk(cols, mean, groups, centered, squares, first):
    for ref, rows, here in groups:
        part = center(ref[rows, cols], mean)
        centered[here, cols] = part
        wide = jnp.square(part.astype(jnp.float32))
        total = wide[:, :LANES]
        for lane in range(LANES, wide.shape[1], LANES):
            total += wide[:, lane : lane + LANES]
        squares[here, :] = total if first else squares[here, :] + total


def add_products(cols, probes, centered, scores, first):
    products = lax.dot_general(
        centered[:, cols], probes[:, cols], (((1,), (1,)), ((), ())),
        preferred_element_type=jnp.float32,
    )
    scores[...] = products if first else scores[...] + products


def log_sum(squares, scores):
    half = 0.5 * jnp.sum(squares[...], axis=1, keepdims=True)
    x = (scores[...] - half) / TEMP
    top = jnp.max(x, axis=0, keepdims=True)
    return jnp.log(jnp.sum(jnp.exp(x - top), axis=0, keepdims=True)) + top


def stage_kernel(queries, own, total):
    total[...] = jnp.sum(own[...].astype(jnp.float32), axis=0, keepdims=True)


def stage(queries, own):
    in_vmem = pl.BlockSpec(memory_space=pltpu.VMEM)
    return pl.pallas_call(
        stage_kernel,
        out_shape=jax.ShapeDtypeStruct((1, own.shape[1]), jnp.float32),
        in_specs=[in_vmem] * 2,
        out_specs=in_vmem,
        compiler_params=pltpu.CompilerParams(vmem_limit_bytes=LIMIT),
        cost_estimate=pl.CostEstimate(
            flops=own.size, bytes_accessed=2 * (queries.size + own.size), transcendentals=0
        ),
    )(queries, own)


def ref_kernel(spans, queries, own_total, *refs):
    panel, (probes, mean, ref_log, centered, squares, scores) = refs[: len(spans)], refs[len(spans) :]
    groups = panel_groups(panel, spans)
    others = [group for group in groups if group[0] is not panel[0]]
    count, features = centered.shape
    for start in range(0, features, CHUNK):
        cols = slice(start, start + CHUNK)
        total = own_total[:, cols]
        for ref, rows, _ in others:
            total += jnp.sum(ref[rows, cols].astype(jnp.float32), axis=0, keepdims=True)
        here = total / count
        mean[:, cols] = here
        center_panel_chunk(cols, here, groups, centered, squares, start == 0)
        for rows in row_groups(probes.shape[0], GROUP):
            probes[rows, cols] = center(queries[rows, cols], here)
        add_products(cols, probes, centered, scores, start == 0)
    ref_log[...] = log_sum(squares, scores)


def gen_kernel(spans, ref_log, probes, mean, *refs):
    panel, (proof, centered, squares, scores) = refs[: len(spans)], refs[len(spans) :]
    groups = panel_groups(panel, spans)
    for start in range(0, centered.shape[1], CHUNK):
        cols = slice(start, start + CHUNK)
        center_panel_chunk(cols, mean[:, cols], groups, centered, squares, start == 0)
        add_products(cols, probes, centered, scores, start == 0)
    proof[...] = log_sum(squares, scores) - ref_log[...]


def call(kernel, before, pieces, count, out_shape):
    spans = [(low, high) for _, low, high in pieces]
    operands = [*before, *(array for array, _, _ in pieces)]
    rows, features = sum(high - low for low, high in spans), operands[-1].shape[1]
    in_vmem = pl.BlockSpec(memory_space=pltpu.VMEM)
    return pl.pallas_call(
        functools.partial(kernel, spans),
        out_shape=out_shape,
        in_specs=[in_vmem] * len(operands),
        out_specs=jax.tree.map(lambda _: in_vmem, out_shape),
        scratch_shapes=[
            pltpu.VMEM((rows, features), jnp.bfloat16),
            pltpu.VMEM((rows, LANES), jnp.float32),
            pltpu.VMEM((rows, count), jnp.float32),
        ],
        compiler_params=pltpu.CompilerParams(vmem_limit_bytes=LIMIT),
        cost_estimate=pl.CostEstimate(
            flops=2 * rows * count * features,
            bytes_accessed=2 * (rows + count) * features,
            transcendentals=rows * count,
        ),
    )(*operands)


def body(queries, gen_panel, ref_panel):
    panels = [ref_panel, gen_panel]
    own_total = stage(queries, ref_panel)
    (ref_pieces, gen_pieces), own_total = gather_panels(panels, own_total, lax.axis_size("samp"))
    count, features = queries.shape
    logs = jax.ShapeDtypeStruct((1, count), jnp.float32)
    probes, mean, ref_log = call(
        ref_kernel,
        [queries, own_total],
        ref_pieces,
        count,
        (
            jax.ShapeDtypeStruct((count, features), jnp.bfloat16),
            jax.ShapeDtypeStruct((1, features), jnp.float32),
            logs,
        ),
    )
    return call(gen_kernel, [ref_log, probes, mean], gen_pieces, count, logs).reshape(-1)


def solution(mesh):
    return jax.shard_map(
        body,
        mesh=mesh,
        in_specs=(
            P(("groups", "samp"), None),
            P(("groups", "samp"), None),
            P(("groups", "samp"), None),
        ),
        out_specs=P(("groups", "samp")),
        check_vma=False,
    )
```

```python
import functools

import jax
import jax.numpy as jnp
from jax import lax
from jax.experimental import pallas as pl
from jax.experimental.pallas import tpu as pltpu
from jax.sharding import PartitionSpec as P

TEMP = 64
LANES = 128
CHUNK = 1024
GROUP = 32
LIMIT = 40 * 2**20


def ring_of_chips(chips):
    return list(range(0, chips, 2)) + list(range(chips - 1 - chips % 2, 0, -2))


def ring_pairs(size):
    order = ring_of_chips(size // 2)
    pairs = []
    for place, chip in enumerate(order):
        after = order[(place + 1) % len(order)]
        before = order[place - 1]
        pairs.append((2 * chip, 2 * after))
        pairs.append((2 * chip + 1, 2 * before + 1))
    return pairs


def core_pairs(size):
    return [(i, i ^ 1) for i in range(size)]


def gather_panels(panels, size, on_first):
    twins, ring = core_pairs(size), ring_pairs(size)
    chips, rows = size // 2, panels[0].shape[0]

    def hop(block):
        return lax.ppermute(block, "samp", ring)

    def hand_over(block):
        return lax.ppermute(block, "samp", twins)

    steps = (chips - 1) // 2
    mine, other = list(panels), None
    pieces = [[] for _ in panels]
    fresh = [[] for _ in panels]
    for period in range(steps + 1):
        last = period == steps
        if last and period:
            mine[-1], extra = lax.optimization_barrier((mine[-1], extra))
        other = [hop(o) for o in other] if period else [hand_over(p) for p in panels]
        if not period:
            extra = on_first(other[0])
        arrived = [[] for _ in panels]
        if not last or chips % 2 == 0:
            mine = [hop(m) for m in mine]
            arrived = [[m] for m in mine]
        for i, o in enumerate(other):
            pieces[i] += [(a, 0, rows) for a in [o] + arrived[i]]
            fresh[i] += [o] + arrived[i]
        if last:
            for i in range(len(panels)):
                if fresh[i]:
                    block = hand_over(jnp.concatenate(fresh[i], axis=0))
                    pieces[i].append((block, 0, block.shape[0]))
        elif period:
            block, at = hand_over(jnp.concatenate([f for g in fresh for f in g], axis=0)), 0
            for i in range(len(panels)):
                upto = at + rows * len(fresh[i])
                pieces[i].append((block, at, upto))
                fresh[i], at = [], upto
    return pieces, extra


def row_groups(rows, step):
    return [slice(r, min(r + step, rows)) for r in range(0, rows, step)]


def panel_groups(refs, spans):
    groups, at = [], 0
    for ref, (low, high) in zip(refs, spans):
        for rows in row_groups(high - low, GROUP):
            size = rows.stop - rows.start
            groups.append((ref, slice(low + rows.start, low + rows.stop), slice(at, at + size)))
            at += size
    return groups


def center(rows, mean):
    return (rows.astype(jnp.float32) - mean).astype(jnp.bfloat16)


def center_panel_chunk(cols, mean, groups, centered, squares, first):
    for ref, rows, here in groups:
        part = center(ref[rows, cols], mean)
        centered[here, cols] = part
        wide = jnp.square(part.astype(jnp.float32))
        total = wide[:, :LANES]
        for lane in range(LANES, wide.shape[1], LANES):
            total += wide[:, lane : lane + LANES]
        squares[here, :] = total if first else squares[here, :] + total


def add_products(cols, probes, centered, scores, first):
    products = lax.dot_general(
        centered[:, cols], probes[:, cols], (((1,), (1,)), ((), ())),
        preferred_element_type=jnp.float32,
    )
    scores[...] = products if first else scores[...] + products


def log_sum(squares, scores):
    half = 0.5 * jnp.sum(squares[...], axis=1, keepdims=True)
    x = (scores[...] - half) / TEMP
    top = jnp.max(x, axis=0, keepdims=True)
    return jnp.log(jnp.sum(jnp.exp(x - top), axis=0, keepdims=True)) + top


def total_kernel(rows, total):
    total[...] = jnp.sum(rows[...].astype(jnp.float32), axis=0, keepdims=True)


def feature_total(rows, beside):
    in_vmem = pl.BlockSpec(memory_space=pltpu.VMEM)
    return pl.pallas_call(
        total_kernel,
        out_shape=jax.ShapeDtypeStruct((1, rows.shape[1]), jnp.float32),
        in_specs=[in_vmem],
        out_specs=in_vmem,
        compiler_params=pltpu.CompilerParams(vmem_limit_bytes=LIMIT),
        cost_estimate=pl.CostEstimate(
            flops=rows.size, bytes_accessed=4 * beside.size, transcendentals=0
        ),
    )(rows)


def ref_kernel(spans, queries, first_total, *refs):
    panel, (probes, mean, ref_log, centered, squares, scores) = refs[: len(spans)], refs[len(spans) :]
    groups = panel_groups(panel, spans)
    count, features = centered.shape
    for start in range(0, features, CHUNK):
        cols = slice(start, start + CHUNK)
        total = first_total[:, cols]
        for ref, rows, _ in groups:
            if ref is not panel[0]:
                total += jnp.sum(ref[rows, cols].astype(jnp.float32), axis=0, keepdims=True)
        here = total / count
        mean[:, cols] = here
        center_panel_chunk(cols, here, groups, centered, squares, start == 0)
        for rows in row_groups(probes.shape[0], GROUP):
            probes[rows, cols] = center(queries[rows, cols], here)
        add_products(cols, probes, centered, scores, start == 0)
    ref_log[...] = log_sum(squares, scores)


def gen_kernel(spans, ref_log, probes, mean, *refs):
    panel, (proof, centered, squares, scores) = refs[: len(spans)], refs[len(spans) :]
    groups = panel_groups(panel, spans)
    for start in range(0, centered.shape[1], CHUNK):
        cols = slice(start, start + CHUNK)
        center_panel_chunk(cols, mean[:, cols], groups, centered, squares, start == 0)
        add_products(cols, probes, centered, scores, start == 0)
    proof[...] = log_sum(squares, scores) - ref_log[...]


def call(kernel, before, pieces, count, out_shape):
    spans = [(low, high) for _, low, high in pieces]
    operands = [*before, *(array for array, _, _ in pieces)]
    rows, features = sum(high - low for low, high in spans), operands[-1].shape[1]
    in_vmem = pl.BlockSpec(memory_space=pltpu.VMEM)
    return pl.pallas_call(
        functools.partial(kernel, spans),
        out_shape=out_shape,
        in_specs=[in_vmem] * len(operands),
        out_specs=jax.tree.map(lambda _: in_vmem, out_shape),
        scratch_shapes=[
            pltpu.VMEM((rows, features), jnp.bfloat16),
            pltpu.VMEM((rows, LANES), jnp.float32),
            pltpu.VMEM((rows, count), jnp.float32),
        ],
        compiler_params=pltpu.CompilerParams(vmem_limit_bytes=LIMIT),
        cost_estimate=pl.CostEstimate(
            flops=2 * rows * count * features,
            bytes_accessed=2 * (rows + count) * features,
            transcendentals=rows * count,
        ),
    )(*operands)


def body(queries, gen_panel, ref_panel):
    panels = [ref_panel, gen_panel]
    (ref_pieces, gen_pieces), first_total = gather_panels(
        panels, lax.axis_size("samp"), functools.partial(feature_total, beside=queries)
    )
    count, features = queries.shape
    logs = jax.ShapeDtypeStruct((1, count), jnp.float32)
    probes, mean, ref_log = call(
        ref_kernel,
        [queries, first_total],
        ref_pieces,
        count,
        (
            jax.ShapeDtypeStruct((count, features), jnp.bfloat16),
            jax.ShapeDtypeStruct((1, features), jnp.float32),
            logs,
        ),
    )
    return call(gen_kernel, [ref_log, probes, mean], gen_pieces, count, logs).reshape(-1)


def solution(mesh):
    return jax.shard_map(
        body,
        mesh=mesh,
        in_specs=(
            P(("groups", "samp"), None),
            P(("groups", "samp"), None),
            P(("groups", "samp"), None),
        ),
        out_specs=P(("groups", "samp")),
        check_vma=False,
    )
```

```python
import functools

import jax
import jax.numpy as jnp
from jax import lax
from jax.experimental import pallas as pl
from jax.experimental.pallas import tpu as pltpu
from jax.sharding import PartitionSpec as P

TEMP = 64
LANES = 128
EIGHT = 8
CHUNK = 1024
GROUP = 32
LIMIT = 40 * 2**20


def ring_of_chips(chips):
    return list(range(0, chips, 2)) + list(range(chips - 1 - chips % 2, 0, -2))


def ring_pairs(size):
    order = ring_of_chips(size // 2)
    pairs = []
    for place, chip in enumerate(order):
        after = order[(place + 1) % len(order)]
        before = order[place - 1]
        pairs.append((2 * chip, 2 * after))
        pairs.append((2 * chip + 1, 2 * before + 1))
    return pairs


def core_pairs(size):
    return [(i, i ^ 1) for i in range(size)]


def gather_panels(panels, size, on_first):
    twins, ring = core_pairs(size), ring_pairs(size)
    chips, rows = size // 2, panels[0].shape[0]

    def hop(block):
        return lax.ppermute(block, "samp", ring)

    def hand_over(block):
        return lax.ppermute(block, "samp", twins)

    steps = (chips - 1) // 2
    mine, other = list(panels), None
    pieces = [[] for _ in panels]
    fresh = [[] for _ in panels]
    for period in range(steps + 1):
        last = period == steps
        if last and period:
            mine[-1], extra = lax.optimization_barrier((mine[-1], extra))
        other = [hop(o) for o in other] if period else [hand_over(p) for p in panels]
        if not period:
            extra = on_first(other[0])
        arrived = [[] for _ in panels]
        if not last or chips % 2 == 0:
            mine = [hop(m) for m in mine]
            arrived = [[m] for m in mine]
        for i, o in enumerate(other):
            pieces[i] += [(a, 0, rows) for a in [o] + arrived[i]]
            fresh[i] += [o] + arrived[i]
        if last:
            for i in range(len(panels)):
                if fresh[i]:
                    block = hand_over(jnp.concatenate(fresh[i], axis=0))
                    pieces[i].append((block, 0, block.shape[0]))
        elif period:
            block, at = hand_over(jnp.concatenate([f for g in fresh for f in g], axis=0)), 0
            for i in range(len(panels)):
                upto = at + rows * len(fresh[i])
                pieces[i].append((block, at, upto))
                fresh[i], at = [], upto
    return pieces, extra


def row_groups(rows, step):
    return [slice(r, min(r + step, rows)) for r in range(0, rows, step)]


def panel_groups(refs, spans):
    groups, at = [], 0
    for ref, (low, high) in zip(refs, spans):
        for rows in row_groups(high - low, GROUP):
            size = rows.stop - rows.start
            groups.append((ref, slice(low + rows.start, low + rows.stop), slice(at, at + size)))
            at += size
    return groups


def center(rows, mean):
    return (rows.astype(jnp.float32) - mean).astype(jnp.bfloat16)


def center_panel_chunk(cols, mean, groups, centered, squares, first):
    for ref, rows, here in groups:
        part = center(ref[rows, cols], mean)
        centered[here, cols] = part
        wide = jnp.square(part.astype(jnp.float32))
        total = wide[:, :LANES]
        for lane in range(LANES, wide.shape[1], LANES):
            total += wide[:, lane : lane + LANES]
        squares[here, :] = total if first else squares[here, :] + total


def add_products(cols, probes, centered, scores, first):
    products = lax.dot_general(
        centered[:, cols], probes[:, cols], (((1,), (1,)), ((), ())),
        preferred_element_type=jnp.float32,
    )
    scores[...] = products if first else scores[...] + products


def log_sum(squares, scores):
    half = 0.5 * jnp.sum(squares[...], axis=1, keepdims=True)
    x = (scores[...] - half) / TEMP
    top = jnp.max(x, axis=0, keepdims=True)
    return jnp.log(jnp.sum(jnp.exp(x - top), axis=0, keepdims=True)) + top


def fold_rows(rows):
    wide = rows.astype(jnp.float32)
    total = wide[:EIGHT]
    for row in range(EIGHT, wide.shape[0], EIGHT):
        total += wide[row : row + EIGHT]
    return total


def total_kernel(rows, total):
    total[...] = fold_rows(rows[...])


def feature_total(rows, beside):
    in_vmem = pl.BlockSpec(memory_space=pltpu.VMEM)
    return pl.pallas_call(
        total_kernel,
        out_shape=jax.ShapeDtypeStruct((EIGHT, rows.shape[1]), jnp.float32),
        in_specs=[in_vmem],
        out_specs=in_vmem,
        compiler_params=pltpu.CompilerParams(vmem_limit_bytes=LIMIT),
        cost_estimate=pl.CostEstimate(
            flops=rows.size, bytes_accessed=4 * beside.size, transcendentals=0
        ),
    )(rows)


def ref_kernel(spans, queries, first_total, *refs):
    panel, (probes, mean, ref_log, centered, squares, scores) = refs[: len(spans)], refs[len(spans) :]
    groups = panel_groups(panel, spans)
    count, features = centered.shape
    for start in range(0, features, CHUNK):
        cols = slice(start, start + CHUNK)
        total = first_total[:, cols]
        for ref, rows, _ in groups:
            if ref is not panel[0]:
                total += fold_rows(ref[rows, cols])
        here = jnp.sum(total, axis=0, keepdims=True) / count
        mean[:, cols] = here
        center_panel_chunk(cols, here, groups, centered, squares, start == 0)
        for rows in row_groups(probes.shape[0], GROUP):
            probes[rows, cols] = center(queries[rows, cols], here)
        add_products(cols, probes, centered, scores, start == 0)
    ref_log[...] = log_sum(squares, scores)


def gen_kernel(spans, ref_log, probes, mean, *refs):
    panel, (proof, centered, squares, scores) = refs[: len(spans)], refs[len(spans) :]
    groups = panel_groups(panel, spans)
    for start in range(0, centered.shape[1], CHUNK):
        cols = slice(start, start + CHUNK)
        center_panel_chunk(cols, mean[:, cols], groups, centered, squares, start == 0)
        add_products(cols, probes, centered, scores, start == 0)
    proof[...] = log_sum(squares, scores) - ref_log[...]


def call(kernel, before, pieces, count, out_shape):
    spans = [(low, high) for _, low, high in pieces]
    operands = [*before, *(array for array, _, _ in pieces)]
    rows, features = sum(high - low for low, high in spans), operands[-1].shape[1]
    in_vmem = pl.BlockSpec(memory_space=pltpu.VMEM)
    return pl.pallas_call(
        functools.partial(kernel, spans),
        out_shape=out_shape,
        in_specs=[in_vmem] * len(operands),
        out_specs=jax.tree.map(lambda _: in_vmem, out_shape),
        scratch_shapes=[
            pltpu.VMEM((rows, features), jnp.bfloat16),
            pltpu.VMEM((rows, LANES), jnp.float32),
            pltpu.VMEM((rows, count), jnp.float32),
        ],
        compiler_params=pltpu.CompilerParams(vmem_limit_bytes=LIMIT),
        cost_estimate=pl.CostEstimate(
            flops=2 * rows * count * features,
            bytes_accessed=2 * (rows + count) * features,
            transcendentals=rows * count,
        ),
    )(*operands)


def body(queries, gen_panel, ref_panel):
    panels = [ref_panel, gen_panel]
    (ref_pieces, gen_pieces), first_total = gather_panels(
        panels, lax.axis_size("samp"), functools.partial(feature_total, beside=queries)
    )
    count, features = queries.shape
    logs = jax.ShapeDtypeStruct((1, count), jnp.float32)
    probes, mean, ref_log = call(
        ref_kernel,
        [queries, first_total],
        ref_pieces,
        count,
        (
            jax.ShapeDtypeStruct((count, features), jnp.bfloat16),
            jax.ShapeDtypeStruct((1, features), jnp.float32),
            logs,
        ),
    )
    return call(gen_kernel, [ref_log, probes, mean], gen_pieces, count, logs).reshape(-1)


def solution(mesh):
    return jax.shard_map(
        body,
        mesh=mesh,
        in_specs=(
            P(("groups", "samp"), None),
            P(("groups", "samp"), None),
            P(("groups", "samp"), None),
        ),
        out_specs=P(("groups", "samp")),
        check_vma=False,
    )
```

```python
import functools

import jax
import jax.numpy as jnp
from jax import lax
from jax.experimental import pallas as pl
from jax.experimental.pallas import tpu as pltpu
from jax.sharding import PartitionSpec as P

TEMP = 64
LANES = 128
CHUNK = 1024
GROUP = 32
LIMIT = 40 * 2**20


def ring_of_chips(chips):
    return list(range(0, chips, 2)) + list(range(chips - 1 - chips % 2, 0, -2))


def ring_pairs(size):
    order = ring_of_chips(size // 2)
    pairs = []
    for place, chip in enumerate(order):
        after = order[(place + 1) % len(order)]
        before = order[place - 1]
        pairs.append((2 * chip, 2 * after))
        pairs.append((2 * chip + 1, 2 * before + 1))
    return pairs


def core_pairs(size):
    return [(i, i ^ 1) for i in range(size)]


def gather_panels(panels, size, on_first):
    twins, ring = core_pairs(size), ring_pairs(size)
    chips, rows = size // 2, panels[0].shape[0]

    def hop(block):
        return lax.ppermute(block, "samp", ring)

    def hand_over(block):
        return lax.ppermute(block, "samp", twins)

    steps = (chips - 1) // 2
    mine, other = list(panels), None
    pieces = [[] for _ in panels]
    fresh = [[] for _ in panels]
    for period in range(steps + 1):
        last = period == steps
        if last and period:
            mine[-1], extra = lax.optimization_barrier((mine[-1], extra))
        other = [hop(o) for o in other] if period else [hand_over(p) for p in panels]
        if not period:
            extra = on_first(other[0])
        arrived = [[] for _ in panels]
        if not last or chips % 2 == 0:
            mine = [hop(m) for m in mine]
            arrived = [[m] for m in mine]
        for i, o in enumerate(other):
            pieces[i] += [(a, 0, rows) for a in [o] + arrived[i]]
            fresh[i] += [o] + arrived[i]
        if last:
            for i in range(len(panels)):
                if fresh[i]:
                    block = hand_over(jnp.concatenate(fresh[i], axis=0))
                    pieces[i].append((block, 0, block.shape[0]))
        elif period:
            block, at = hand_over(jnp.concatenate([f for g in fresh for f in g], axis=0)), 0
            for i in range(len(panels)):
                upto = at + rows * len(fresh[i])
                pieces[i].append((block, at, upto))
                fresh[i], at = [], upto
    return pieces, extra


def row_groups(rows, step):
    return [slice(r, min(r + step, rows)) for r in range(0, rows, step)]


def panel_groups(refs, spans):
    groups, at = [], 0
    for ref, (low, high) in zip(refs, spans):
        for rows in row_groups(high - low, GROUP):
            size = rows.stop - rows.start
            groups.append((ref, slice(low + rows.start, low + rows.stop), slice(at, at + size)))
            at += size
    return groups


def center(rows, mean):
    return (rows.astype(jnp.float32) - mean).astype(jnp.bfloat16)


def center_panel_chunk(cols, mean, groups, centered, squares, first):
    for ref, rows, here in groups:
        part = center(ref[rows, cols], mean)
        centered[here, cols] = part
        wide = jnp.square(part.astype(jnp.float32))
        total = wide[:, :LANES]
        for lane in range(LANES, wide.shape[1], LANES):
            total += wide[:, lane : lane + LANES]
        squares[here, :] = total if first else squares[here, :] + total


def add_products(cols, probes, centered, scores, first):
    products = lax.dot_general(
        probes[:, cols], centered[:, cols], (((1,), (1,)), ((), ())),
        preferred_element_type=jnp.float32,
    )
    scores[...] = products if first else scores[...] + products


def log_sum(squares, scores):
    half = 0.5 * jnp.sum(squares[...].T, axis=0, keepdims=True)
    x = (scores[...] - half) / TEMP
    top = jnp.max(x, axis=1, keepdims=True)
    return jnp.log(jnp.sum(jnp.exp(x - top), axis=1, keepdims=True)) + top


def total_kernel(rows, total):
    total[...] = jnp.sum(rows[...].astype(jnp.float32), axis=0, keepdims=True)


def feature_total(rows, beside):
    in_vmem = pl.BlockSpec(memory_space=pltpu.VMEM)
    return pl.pallas_call(
        total_kernel,
        out_shape=jax.ShapeDtypeStruct((1, rows.shape[1]), jnp.float32),
        in_specs=[in_vmem],
        out_specs=in_vmem,
        compiler_params=pltpu.CompilerParams(vmem_limit_bytes=LIMIT),
        cost_estimate=pl.CostEstimate(
            flops=rows.size, bytes_accessed=4 * beside.size, transcendentals=0
        ),
    )(rows)


def ref_kernel(spans, queries, first_total, *refs):
    panel, (probes, mean, ref_log, centered, squares, scores) = refs[: len(spans)], refs[len(spans) :]
    groups = panel_groups(panel, spans)
    count, features = centered.shape
    for start in range(0, features, CHUNK):
        cols = slice(start, start + CHUNK)
        total = first_total[:, cols]
        for ref, rows, _ in groups:
            if ref is not panel[0]:
                total += jnp.sum(ref[rows, cols].astype(jnp.float32), axis=0, keepdims=True)
        here = total / count
        mean[:, cols] = here
        center_panel_chunk(cols, here, groups, centered, squares, start == 0)
        for rows in row_groups(probes.shape[0], GROUP):
            probes[rows, cols] = center(queries[rows, cols], here)
        add_products(cols, probes, centered, scores, start == 0)
    ref_log[...] = log_sum(squares, scores)


def gen_kernel(spans, ref_log, probes, mean, *refs):
    panel, (proof, centered, squares, scores) = refs[: len(spans)], refs[len(spans) :]
    groups = panel_groups(panel, spans)
    for start in range(0, centered.shape[1], CHUNK):
        cols = slice(start, start + CHUNK)
        center_panel_chunk(cols, mean[:, cols], groups, centered, squares, start == 0)
        add_products(cols, probes, centered, scores, start == 0)
    column = log_sum(squares, scores) - ref_log[...]
    proof[...] = jnp.broadcast_to(column, (column.shape[0], LANES)).T[:1]


def call(kernel, before, pieces, count, out_shape):
    spans = [(low, high) for _, low, high in pieces]
    operands = [*before, *(array for array, _, _ in pieces)]
    rows, features = sum(high - low for low, high in spans), operands[-1].shape[1]
    in_vmem = pl.BlockSpec(memory_space=pltpu.VMEM)
    return pl.pallas_call(
        functools.partial(kernel, spans),
        out_shape=out_shape,
        in_specs=[in_vmem] * len(operands),
        out_specs=jax.tree.map(lambda _: in_vmem, out_shape),
        scratch_shapes=[
            pltpu.VMEM((rows, features), jnp.bfloat16),
            pltpu.VMEM((rows, LANES), jnp.float32),
            pltpu.VMEM((count, rows), jnp.float32),
        ],
        compiler_params=pltpu.CompilerParams(vmem_limit_bytes=LIMIT),
        cost_estimate=pl.CostEstimate(
            flops=2 * rows * count * features,
            bytes_accessed=2 * (rows + count) * features,
            transcendentals=rows * count,
        ),
    )(*operands)


def body(queries, gen_panel, ref_panel):
    panels = [ref_panel, gen_panel]
    (ref_pieces, gen_pieces), first_total = gather_panels(
        panels, lax.axis_size("samp"), functools.partial(feature_total, beside=queries)
    )
    count, features = queries.shape
    column, row = (jax.ShapeDtypeStruct(s, jnp.float32) for s in ((count, 1), (1, count)))
    probes, mean, ref_log = call(
        ref_kernel,
        [queries, first_total],
        ref_pieces,
        count,
        (
            jax.ShapeDtypeStruct((count, features), jnp.bfloat16),
            jax.ShapeDtypeStruct((1, features), jnp.float32),
            column,
        ),
    )
    return call(gen_kernel, [ref_log, probes, mean], gen_pieces, count, row).reshape(-1)


def solution(mesh):
    return jax.shard_map(
        body,
        mesh=mesh,
        in_specs=(
            P(("groups", "samp"), None),
            P(("groups", "samp"), None),
            P(("groups", "samp"), None),
        ),
        out_specs=P(("groups", "samp")),
        check_vma=False,
    )
```

```python
import functools

import jax
import jax.numpy as jnp
from jax import lax
from jax.experimental import pallas as pl
from jax.experimental.pallas import tpu as pltpu
from jax.sharding import PartitionSpec as P

TEMP = 64
LANES = 128
CHUNK = 1024
GROUP = 32
BLOCK = 256
LIMIT = 40 * 2**20


def ring_of_chips(chips):
    return list(range(0, chips, 2)) + list(range(chips - 1 - chips % 2, 0, -2))


def ring_pairs(size):
    order = ring_of_chips(size // 2)
    pairs = []
    for place, chip in enumerate(order):
        after = order[(place + 1) % len(order)]
        before = order[place - 1]
        pairs.append((2 * chip, 2 * after))
        pairs.append((2 * chip + 1, 2 * before + 1))
    return pairs


def core_pairs(size):
    return [(i, i ^ 1) for i in range(size)]


def gather_panels(panels, size, on_first):
    twins, ring = core_pairs(size), ring_pairs(size)
    chips, rows = size // 2, panels[0].shape[0]

    def hop(block):
        return lax.ppermute(block, "samp", ring)

    def hand_over(block):
        return lax.ppermute(block, "samp", twins)

    steps = (chips - 1) // 2
    mine, other = list(panels), None
    pieces = [[] for _ in panels]
    fresh = [[] for _ in panels]
    for period in range(steps + 1):
        last = period == steps
        if last and period:
            mine[-1], extra = lax.optimization_barrier((mine[-1], extra))
        other = [hop(o) for o in other] if period else [hand_over(p) for p in panels]
        if not period:
            extra = on_first(other[0])
        arrived = [[] for _ in panels]
        if not last or chips % 2 == 0:
            mine = [hop(m) for m in mine]
            arrived = [[m] for m in mine]
        for i, o in enumerate(other):
            pieces[i] += [(a, 0, rows) for a in [o] + arrived[i]]
            fresh[i] += [o] + arrived[i]
        if last:
            for i in range(len(panels)):
                if fresh[i]:
                    block = hand_over(jnp.concatenate(fresh[i], axis=0))
                    pieces[i].append((block, 0, block.shape[0]))
        elif period:
            block, at = hand_over(jnp.concatenate([f for g in fresh for f in g], axis=0)), 0
            for i in range(len(panels)):
                upto = at + rows * len(fresh[i])
                pieces[i].append((block, at, upto))
                fresh[i], at = [], upto
    return pieces, extra


def row_groups(rows, step):
    return [slice(r, min(r + step, rows)) for r in range(0, rows, step)]


def panel_groups(refs, spans):
    groups, at = [], 0
    for ref, (low, high) in zip(refs, spans):
        for rows in row_groups(high - low, GROUP):
            size = rows.stop - rows.start
            groups.append((ref, slice(low + rows.start, low + rows.stop), slice(at, at + size)))
            at += size
    return groups


def center(rows, mean):
    return (rows.astype(jnp.float32) - mean).astype(jnp.bfloat16)


def center_group(group, cols, mean, centered, squares, first):
    ref, rows, here = group
    part = center(ref[rows, cols], mean[:, cols])
    centered[here, cols] = part
    wide = jnp.square(part.astype(jnp.float32))
    total = wide[:, :LANES]
    for lane in range(LANES, wide.shape[1], LANES):
        total += wide[:, lane : lane + LANES]
    squares[here, :] = total if first else squares[here, :] + total


def add_products(cols, queries, probes, centered, scores, first):
    products = lax.dot_general(
        centered[:, cols], probes[queries, cols], (((1,), (1,)), ((), ())),
        preferred_element_type=jnp.float32,
    )
    scores[:, queries] = products if first else scores[:, queries] + products


def interleave(features, prepare, probes, centered, scores):
    waiting = []
    for start in range(0, features, CHUNK):
        cols, first = slice(start, start + CHUNK), start == 0
        work = prepare(cols, first)
        share = -(-len(work) // max(len(waiting), 1))
        for i in range(0, len(work), share):
            if waiting:
                waiting.pop(0)()
            for step in work[i : i + share]:
                step()
        waiting += [
            functools.partial(add_products, cols, queries, probes, centered, scores, first)
            for queries in row_groups(probes.shape[0], BLOCK)
        ]
    for step in waiting:
        step()


def log_sum(squares, scores, queries):
    half = 0.5 * jnp.sum(squares[...], axis=1, keepdims=True)
    x = (scores[:, queries] - half) / TEMP
    top = jnp.max(x, axis=0, keepdims=True)
    return jnp.log(jnp.sum(jnp.exp(x - top), axis=0, keepdims=True)) + top


def total_kernel(rows, total):
    total[...] = jnp.sum(rows[...].astype(jnp.float32), axis=0, keepdims=True)


def feature_total(rows, beside):
    in_vmem = pl.BlockSpec(memory_space=pltpu.VMEM)
    return pl.pallas_call(
        total_kernel,
        out_shape=jax.ShapeDtypeStruct((1, rows.shape[1]), jnp.float32),
        in_specs=[in_vmem],
        out_specs=in_vmem,
        compiler_params=pltpu.CompilerParams(vmem_limit_bytes=LIMIT),
        cost_estimate=pl.CostEstimate(
            flops=rows.size, bytes_accessed=4 * beside.size, transcendentals=0
        ),
    )(rows)


def ref_kernel(spans, queries, first_total, *refs):
    panel, (probes, mean, ref_log, centered, squares, scores) = refs[: len(spans)], refs[len(spans) :]
    groups = panel_groups(panel, spans)
    count, features = centered.shape

    def take_mean(cols):
        total = first_total[:, cols]
        for ref, rows, _ in groups:
            if ref is not panel[0]:
                total += jnp.sum(ref[rows, cols].astype(jnp.float32), axis=0, keepdims=True)
        mean[:, cols] = total / count

    def center_queries(rows, cols):
        probes[rows, cols] = center(queries[rows, cols], mean[:, cols])

    def prepare(cols, first):
        work = [functools.partial(take_mean, cols)]
        for group in groups:
            work.append(functools.partial(center_group, group, cols, mean, centered, squares, first))
        for rows in row_groups(probes.shape[0], GROUP):
            work.append(functools.partial(center_queries, rows, cols))
        return work

    interleave(features, prepare, probes, centered, scores)
    for block in row_groups(probes.shape[0], BLOCK):
        ref_log[:, block] = log_sum(squares, scores, block)


def gen_kernel(spans, ref_log, probes, mean, *refs):
    panel, (proof, centered, squares, scores) = refs[: len(spans)], refs[len(spans) :]
    groups = panel_groups(panel, spans)

    def prepare(cols, first):
        return [
            functools.partial(center_group, group, cols, mean, centered, squares, first)
            for group in groups
        ]

    interleave(centered.shape[1], prepare, probes, centered, scores)
    for block in row_groups(probes.shape[0], BLOCK):
        proof[:, block] = log_sum(squares, scores, block) - ref_log[:, block]


def call(kernel, before, pieces, count, out_shape):
    spans = [(low, high) for _, low, high in pieces]
    operands = [*before, *(array for array, _, _ in pieces)]
    rows, features = sum(high - low for low, high in spans), operands[-1].shape[1]
    in_vmem = pl.BlockSpec(memory_space=pltpu.VMEM)
    return pl.pallas_call(
        functools.partial(kernel, spans),
        out_shape=out_shape,
        in_specs=[in_vmem] * len(operands),
        out_specs=jax.tree.map(lambda _: in_vmem, out_shape),
        scratch_shapes=[
            pltpu.VMEM((rows, features), jnp.bfloat16),
            pltpu.VMEM((rows, LANES), jnp.float32),
            pltpu.VMEM((rows, count), jnp.float32),
        ],
        compiler_params=pltpu.CompilerParams(vmem_limit_bytes=LIMIT),
        cost_estimate=pl.CostEstimate(
            flops=2 * rows * count * features,
            bytes_accessed=2 * (rows + count) * features,
            transcendentals=rows * count,
        ),
    )(*operands)


def body(queries, gen_panel, ref_panel):
    panels = [ref_panel, gen_panel]
    (ref_pieces, gen_pieces), first_total = gather_panels(
        panels, lax.axis_size("samp"), functools.partial(feature_total, beside=queries)
    )
    count, features = queries.shape
    logs = jax.ShapeDtypeStruct((1, count), jnp.float32)
    probes, mean, ref_log = call(
        ref_kernel,
        [queries, first_total],
        ref_pieces,
        count,
        (
            jax.ShapeDtypeStruct((count, features), jnp.bfloat16),
            jax.ShapeDtypeStruct((1, features), jnp.float32),
            logs,
        ),
    )
    return call(gen_kernel, [ref_log, probes, mean], gen_pieces, count, logs).reshape(-1)


def solution(mesh):
    return jax.shard_map(
        body,
        mesh=mesh,
        in_specs=(
            P(("groups", "samp"), None),
            P(("groups", "samp"), None),
            P(("groups", "samp"), None),
        ),
        out_specs=P(("groups", "samp")),
        check_vma=False,
    )
```

```python
import functools

import jax
import jax.numpy as jnp
from jax import lax
from jax.experimental import pallas as pl
from jax.experimental.pallas import tpu as pltpu
from jax.sharding import PartitionSpec as P

TEMP = 64
LANES = 128
CHUNK = 1024
GROUP = 32
BLOCK = 256
LIMIT = 40 * 2**20


def ring_of_chips(chips):
    return list(range(0, chips, 2)) + list(range(chips - 1 - chips % 2, 0, -2))


def ring_pairs(size):
    order = ring_of_chips(size // 2)
    pairs = []
    for place, chip in enumerate(order):
        after = order[(place + 1) % len(order)]
        before = order[place - 1]
        pairs.append((2 * chip, 2 * after))
        pairs.append((2 * chip + 1, 2 * before + 1))
    return pairs


def core_pairs(size):
    return [(i, i ^ 1) for i in range(size)]


def gather_panels(panels, size, on_first):
    twins, ring = core_pairs(size), ring_pairs(size)
    chips, rows = size // 2, panels[0].shape[0]

    def hop(block):
        return lax.ppermute(block, "samp", ring)

    def hand_over(block):
        return lax.ppermute(block, "samp", twins)

    steps = (chips - 1) // 2
    mine, other = list(panels), None
    pieces = [[] for _ in panels]
    fresh = [[] for _ in panels]
    for period in range(steps + 1):
        last = period == steps
        if last and period:
            mine[-1], extra = lax.optimization_barrier((mine[-1], extra))
        other = [hop(o) for o in other] if period else [hand_over(p) for p in panels]
        if not period:
            extra = on_first(other[0])
        arrived = [[] for _ in panels]
        if not last or chips % 2 == 0:
            mine = [hop(m) for m in mine]
            arrived = [[m] for m in mine]
        for i, o in enumerate(other):
            pieces[i] += [(a, 0, rows) for a in [o] + arrived[i]]
            fresh[i] += [o] + arrived[i]
        if last:
            for i in range(len(panels)):
                if fresh[i]:
                    block = hand_over(jnp.concatenate(fresh[i], axis=0))
                    pieces[i].append((block, 0, block.shape[0]))
        elif period:
            block, at = hand_over(jnp.concatenate([f for g in fresh for f in g], axis=0)), 0
            for i in range(len(panels)):
                upto = at + rows * len(fresh[i])
                pieces[i].append((block, at, upto))
                fresh[i], at = [], upto
    return pieces, extra


def row_groups(rows, step):
    return [slice(r, min(r + step, rows)) for r in range(0, rows, step)]


def panel_groups(refs, spans):
    groups, at = [], 0
    for ref, (low, high) in zip(refs, spans):
        for rows in row_groups(high - low, GROUP):
            size = rows.stop - rows.start
            groups.append((ref, slice(low + rows.start, low + rows.stop), slice(at, at + size)))
            at += size
    return groups


def center(rows, mean):
    return (rows.astype(jnp.float32) - mean).astype(jnp.bfloat16)


def center_group(group, cols, mean, centered, squares, first):
    ref, rows, here = group
    part = center(ref[rows, cols], mean[:, cols])
    centered[here, cols] = part
    wide = jnp.square(part.astype(jnp.float32))
    total = wide[:, :LANES]
    for lane in range(LANES, wide.shape[1], LANES):
        total += wide[:, lane : lane + LANES]
    squares[here, :] = total if first else squares[here, :] + total


def add_log_sums(probes, centered, squares, scores, store):
    for queries in row_groups(probes.shape[0], BLOCK):
        scores[:, queries] = lax.dot_general(
            centered[...], probes[queries, :], (((1,), (1,)), ((), ())),
            preferred_element_type=jnp.float32,
        )
    for queries in row_groups(probes.shape[0], BLOCK):
        store(queries, log_sum(squares, scores, queries))


def log_sum(squares, scores, queries):
    half = 0.5 * jnp.sum(squares[...], axis=1, keepdims=True)
    x = (scores[:, queries] - half) / TEMP
    top = jnp.max(x, axis=0, keepdims=True)
    return jnp.log(jnp.sum(jnp.exp(x - top), axis=0, keepdims=True)) + top


def total_kernel(rows, total):
    total[...] = jnp.sum(rows[...].astype(jnp.float32), axis=0, keepdims=True)


def feature_total(rows, beside):
    in_vmem = pl.BlockSpec(memory_space=pltpu.VMEM)
    return pl.pallas_call(
        total_kernel,
        out_shape=jax.ShapeDtypeStruct((1, rows.shape[1]), jnp.float32),
        in_specs=[in_vmem],
        out_specs=in_vmem,
        compiler_params=pltpu.CompilerParams(vmem_limit_bytes=LIMIT),
        cost_estimate=pl.CostEstimate(
            flops=rows.size, bytes_accessed=4 * beside.size, transcendentals=0
        ),
    )(rows)


def ref_kernel(spans, queries, first_total, *refs):
    panel, (probes, mean, ref_log, centered, squares, scores) = refs[: len(spans)], refs[len(spans) :]
    groups = panel_groups(panel, spans)
    count, features = centered.shape

    def take_mean(cols):
        total = first_total[:, cols]
        for ref, rows, _ in groups:
            if ref is not panel[0]:
                total += jnp.sum(ref[rows, cols].astype(jnp.float32), axis=0, keepdims=True)
        mean[:, cols] = total / count

    def center_queries(rows, cols):
        probes[rows, cols] = center(queries[rows, cols], mean[:, cols])

    for start in range(0, features, CHUNK):
        cols = slice(start, start + CHUNK)
        take_mean(cols)
        for group in groups:
            center_group(group, cols, mean, centered, squares, start == 0)
        for rows in row_groups(probes.shape[0], GROUP):
            center_queries(rows, cols)

    def store(block, value):
        ref_log[:, block] = value

    add_log_sums(probes, centered, squares, scores, store)


def gen_kernel(spans, ref_log, probes, mean, *refs):
    panel, (proof, centered, squares, scores) = refs[: len(spans)], refs[len(spans) :]
    groups = panel_groups(panel, spans)

    for start in range(0, centered.shape[1], CHUNK):
        for group in groups:
            center_group(group, slice(start, start + CHUNK), mean, centered, squares, start == 0)

    def store(block, value):
        proof[:, block] = value - ref_log[:, block]

    add_log_sums(probes, centered, squares, scores, store)


def call(kernel, before, pieces, count, out_shape):
    spans = [(low, high) for _, low, high in pieces]
    operands = [*before, *(array for array, _, _ in pieces)]
    rows, features = sum(high - low for low, high in spans), operands[-1].shape[1]
    in_vmem = pl.BlockSpec(memory_space=pltpu.VMEM)
    return pl.pallas_call(
        functools.partial(kernel, spans),
        out_shape=out_shape,
        in_specs=[in_vmem] * len(operands),
        out_specs=jax.tree.map(lambda _: in_vmem, out_shape),
        scratch_shapes=[
            pltpu.VMEM((rows, features), jnp.bfloat16),
            pltpu.VMEM((rows, LANES), jnp.float32),
            pltpu.VMEM((rows, count), jnp.float32),
        ],
        compiler_params=pltpu.CompilerParams(vmem_limit_bytes=LIMIT),
        cost_estimate=pl.CostEstimate(
            flops=2 * rows * count * features,
            bytes_accessed=2 * (rows + count) * features,
            transcendentals=rows * count,
        ),
    )(*operands)


def body(queries, gen_panel, ref_panel):
    panels = [ref_panel, gen_panel]
    (ref_pieces, gen_pieces), first_total = gather_panels(
        panels, lax.axis_size("samp"), functools.partial(feature_total, beside=queries)
    )
    count, features = queries.shape
    logs = jax.ShapeDtypeStruct((1, count), jnp.float32)
    probes, mean, ref_log = call(
        ref_kernel,
        [queries, first_total],
        ref_pieces,
        count,
        (
            jax.ShapeDtypeStruct((count, features), jnp.bfloat16),
            jax.ShapeDtypeStruct((1, features), jnp.float32),
            logs,
        ),
    )
    return call(gen_kernel, [ref_log, probes, mean], gen_pieces, count, logs).reshape(-1)


def solution(mesh):
    return jax.shard_map(
        body,
        mesh=mesh,
        in_specs=(
            P(("groups", "samp"), None),
            P(("groups", "samp"), None),
            P(("groups", "samp"), None),
        ),
        out_specs=P(("groups", "samp")),
        check_vma=False,
    )
```

```python
import functools

import jax
import jax.numpy as jnp
from jax import lax
from jax.experimental import pallas as pl
from jax.experimental.pallas import tpu as pltpu
from jax.sharding import PartitionSpec as P

TEMP = 64
LANES = 128
CHUNK = 1024
GROUP = 32
BLOCK = 256
LIMIT = 40 * 2**20


def ring_of_chips(chips):
    return list(range(0, chips, 2)) + list(range(chips - 1 - chips % 2, 0, -2))


def ring_pairs(size):
    order = ring_of_chips(size // 2)
    pairs = []
    for place, chip in enumerate(order):
        after = order[(place + 1) % len(order)]
        before = order[place - 1]
        pairs.append((2 * chip, 2 * after))
        pairs.append((2 * chip + 1, 2 * before + 1))
    return pairs


def core_pairs(size):
    return [(i, i ^ 1) for i in range(size)]


def gather_panels(panels, size, on_first):
    twins, ring = core_pairs(size), ring_pairs(size)
    chips, rows = size // 2, panels[0].shape[0]

    def hop(block):
        return lax.ppermute(block, "samp", ring)

    def hand_over(block):
        return lax.ppermute(block, "samp", twins)

    steps = (chips - 1) // 2
    mine, other = list(panels), None
    pieces = [[] for _ in panels]
    fresh = [[] for _ in panels]
    for period in range(steps + 1):
        last = period == steps
        if last and period:
            other[0], extra = lax.optimization_barrier((other[0], extra))
        other = [hop(o) for o in other] if period else [hand_over(p) for p in panels]
        if not period:
            extra = on_first(other[0])
        arrived = [[] for _ in panels]
        if not last or chips % 2 == 0:
            mine = [hop(m) for m in mine]
            arrived = [[m] for m in mine]
        for i, o in enumerate(other):
            pieces[i] += [(a, 0, rows) for a in [o] + arrived[i]]
            fresh[i] += [o] + arrived[i]
        if last:
            for i in range(len(panels)):
                if fresh[i]:
                    block = hand_over(jnp.concatenate(fresh[i], axis=0))
                    pieces[i].append((block, 0, block.shape[0]))
        elif period and period < steps - 1:
            block, at = hand_over(jnp.concatenate([f for g in fresh for f in g], axis=0)), 0
            for i in range(len(panels)):
                upto = at + rows * len(fresh[i])
                pieces[i].append((block, at, upto))
                fresh[i], at = [], upto
    return pieces, extra


def row_groups(rows, step):
    return [slice(r, min(r + step, rows)) for r in range(0, rows, step)]


def panel_groups(refs, spans):
    groups, at = [], 0
    for ref, (low, high) in zip(refs, spans):
        for rows in row_groups(high - low, GROUP):
            size = rows.stop - rows.start
            groups.append((ref, slice(low + rows.start, low + rows.stop), slice(at, at + size)))
            at += size
    return groups


def center(rows, mean):
    return (rows.astype(jnp.float32) - mean).astype(jnp.bfloat16)


def center_group(group, cols, mean, centered, squares, first):
    ref, rows, here = group
    part = center(ref[rows, cols], mean[:, cols])
    centered[here, cols] = part
    wide = jnp.square(part.astype(jnp.float32))
    total = wide[:, :LANES]
    for lane in range(LANES, wide.shape[1], LANES):
        total += wide[:, lane : lane + LANES]
    squares[here, :] = total if first else squares[here, :] + total


def add_products(cols, queries, probes, centered, scores, first):
    products = lax.dot_general(
        centered[:, cols], probes[queries, cols], (((1,), (1,)), ((), ())),
        preferred_element_type=jnp.float32,
    )
    scores[:, queries] = products if first else scores[:, queries] + products


def interleave(features, prepare, probes, centered, scores):
    waiting = []
    for start in range(0, features, CHUNK):
        cols, first = slice(start, start + CHUNK), start == 0
        work = prepare(cols, first)
        share = -(-len(work) // max(len(waiting), 1))
        for i in range(0, len(work), share):
            if waiting:
                waiting.pop(0)()
            for step in work[i : i + share]:
                step()
        waiting += [
            functools.partial(add_products, cols, queries, probes, centered, scores, first)
            for queries in row_groups(probes.shape[0], BLOCK)
        ]
    for step in waiting:
        step()


def log_sum(squares, scores, queries):
    half = 0.5 * jnp.sum(squares[...], axis=1, keepdims=True)
    x = (scores[:, queries] - half) / TEMP
    top = jnp.max(x, axis=0, keepdims=True)
    return jnp.log(jnp.sum(jnp.exp(x - top), axis=0, keepdims=True)) + top


def total_kernel(rows, total):
    total[...] = jnp.sum(rows[...].astype(jnp.float32), axis=0, keepdims=True)


def feature_total(rows, beside):
    in_vmem = pl.BlockSpec(memory_space=pltpu.VMEM)
    return pl.pallas_call(
        total_kernel,
        out_shape=jax.ShapeDtypeStruct((1, rows.shape[1]), jnp.float32),
        in_specs=[in_vmem],
        out_specs=in_vmem,
        compiler_params=pltpu.CompilerParams(vmem_limit_bytes=LIMIT),
        cost_estimate=pl.CostEstimate(
            flops=rows.size, bytes_accessed=4 * beside.size, transcendentals=0
        ),
    )(rows)


def ref_kernel(spans, queries, first_total, *refs):
    panel, (probes, mean, ref_log, centered, squares, scores) = refs[: len(spans)], refs[len(spans) :]
    groups = panel_groups(panel, spans)
    count, features = centered.shape

    def take_mean(cols):
        total = first_total[:, cols]
        for ref, rows, _ in groups:
            if ref is not panel[0]:
                total += jnp.sum(ref[rows, cols].astype(jnp.float32), axis=0, keepdims=True)
        mean[:, cols] = total / count

    def center_queries(rows, cols):
        probes[rows, cols] = center(queries[rows, cols], mean[:, cols])

    def prepare(cols, first):
        work = [functools.partial(take_mean, cols)]
        for group in groups:
            work.append(functools.partial(center_group, group, cols, mean, centered, squares, first))
        for rows in row_groups(probes.shape[0], GROUP):
            work.append(functools.partial(center_queries, rows, cols))
        return work

    interleave(features, prepare, probes, centered, scores)
    for block in row_groups(probes.shape[0], BLOCK):
        ref_log[:, block] = log_sum(squares, scores, block)


def gen_kernel(spans, ref_log, probes, mean, *refs):
    panel, (proof, centered, squares, scores) = refs[: len(spans)], refs[len(spans) :]
    groups = panel_groups(panel, spans)

    def prepare(cols, first):
        return [
            functools.partial(center_group, group, cols, mean, centered, squares, first)
            for group in groups
        ]

    interleave(centered.shape[1], prepare, probes, centered, scores)
    for block in row_groups(probes.shape[0], BLOCK):
        proof[:, block] = log_sum(squares, scores, block) - ref_log[:, block]


def call(kernel, before, pieces, count, out_shape):
    spans = [(low, high) for _, low, high in pieces]
    operands = [*before, *(array for array, _, _ in pieces)]
    rows, features = sum(high - low for low, high in spans), operands[-1].shape[1]
    in_vmem = pl.BlockSpec(memory_space=pltpu.VMEM)
    return pl.pallas_call(
        functools.partial(kernel, spans),
        out_shape=out_shape,
        in_specs=[in_vmem] * len(operands),
        out_specs=jax.tree.map(lambda _: in_vmem, out_shape),
        scratch_shapes=[
            pltpu.VMEM((rows, features), jnp.bfloat16),
            pltpu.VMEM((rows, LANES), jnp.float32),
            pltpu.VMEM((rows, count), jnp.float32),
        ],
        compiler_params=pltpu.CompilerParams(vmem_limit_bytes=LIMIT),
        cost_estimate=pl.CostEstimate(
            flops=2 * rows * count * features,
            bytes_accessed=2 * (rows + count) * features,
            transcendentals=rows * count,
        ),
    )(*operands)


def body(queries, gen_panel, ref_panel):
    panels = [ref_panel, gen_panel]
    (ref_pieces, gen_pieces), first_total = gather_panels(
        panels, lax.axis_size("samp"), functools.partial(feature_total, beside=queries)
    )
    count, features = queries.shape
    logs = jax.ShapeDtypeStruct((1, count), jnp.float32)
    probes, mean, ref_log = call(
        ref_kernel,
        [queries, first_total],
        ref_pieces,
        count,
        (
            jax.ShapeDtypeStruct((count, features), jnp.bfloat16),
            jax.ShapeDtypeStruct((1, features), jnp.float32),
            logs,
        ),
    )
    return call(gen_kernel, [ref_log, probes, mean], gen_pieces, count, logs).reshape(-1)


def solution(mesh):
    return jax.shard_map(
        body,
        mesh=mesh,
        in_specs=(
            P(("groups", "samp"), None),
            P(("groups", "samp"), None),
            P(("groups", "samp"), None),
        ),
        out_specs=P(("groups", "samp")),
        check_vma=False,
    )
```

```python
import functools

import jax
import jax.numpy as jnp
from jax import lax
from jax.experimental import pallas as pl
from jax.experimental.pallas import tpu as pltpu
from jax.sharding import PartitionSpec as P

TEMP = 64
LANES = 128
CHUNK = 512
GROUP = 16
BLOCK = 256
LIMIT = 40 * 2**20


def ring_of_chips(chips):
    return list(range(0, chips, 2)) + list(range(chips - 1 - chips % 2, 0, -2))


def ring_pairs(size):
    order = ring_of_chips(size // 2)
    pairs = []
    for place, chip in enumerate(order):
        after = order[(place + 1) % len(order)]
        before = order[place - 1]
        pairs.append((2 * chip, 2 * after))
        pairs.append((2 * chip + 1, 2 * before + 1))
    return pairs


def core_pairs(size):
    return [(i, i ^ 1) for i in range(size)]


def gather_panels(panels, size, on_first):
    twins, ring = core_pairs(size), ring_pairs(size)
    chips, rows = size // 2, panels[0].shape[0]

    def hop(block):
        return lax.ppermute(block, "samp", ring)

    def hand_over(block):
        return lax.ppermute(block, "samp", twins)

    steps = (chips - 1) // 2
    mine, other = list(panels), None
    pieces = [[] for _ in panels]
    fresh = [[] for _ in panels]
    for period in range(steps + 1):
        last = period == steps
        if last and period:
            other[0], extra = lax.optimization_barrier((other[0], extra))
        other = [hop(o) for o in other] if period else [hand_over(p) for p in panels]
        if not period:
            extra = on_first(other[0])
        arrived = [[] for _ in panels]
        if not last or chips % 2 == 0:
            mine = [hop(m) for m in mine]
            arrived = [[m] for m in mine]
        for i, o in enumerate(other):
            pieces[i] += [(a, 0, rows) for a in [o] + arrived[i]]
            fresh[i] += [o] + arrived[i]
        if last:
            for i in range(len(panels)):
                if fresh[i]:
                    block = hand_over(jnp.concatenate(fresh[i], axis=0))
                    pieces[i].append((block, 0, block.shape[0]))
        elif period and period < steps - 1:
            block, at = hand_over(jnp.concatenate([f for g in fresh for f in g], axis=0)), 0
            for i in range(len(panels)):
                upto = at + rows * len(fresh[i])
                pieces[i].append((block, at, upto))
                fresh[i], at = [], upto
    return pieces, extra


def row_groups(rows, step):
    return [slice(r, min(r + step, rows)) for r in range(0, rows, step)]


def panel_groups(refs, spans):
    groups, at = [], 0
    for ref, (low, high) in zip(refs, spans):
        for rows in row_groups(high - low, GROUP):
            size = rows.stop - rows.start
            groups.append((ref, slice(low + rows.start, low + rows.stop), slice(at, at + size)))
            at += size
    return groups


def center(rows, mean):
    return (rows.astype(jnp.float32) - mean).astype(jnp.bfloat16)


def center_group(group, cols, mean, centered, squares, first):
    ref, rows, here = group
    part = center(ref[rows, cols], mean[:, cols])
    centered[here, cols] = part
    wide = jnp.square(part.astype(jnp.float32))
    total = wide[:, :LANES]
    for lane in range(LANES, wide.shape[1], LANES):
        total += wide[:, lane : lane + LANES]
    squares[here, :] = total if first else squares[here, :] + total


def add_products(cols, queries, probes, centered, scores, first):
    products = lax.dot_general(
        centered[:, cols], probes[queries, cols], (((1,), (1,)), ((), ())),
        preferred_element_type=jnp.float32,
    )
    scores[:, queries] = products if first else scores[:, queries] + products


def interleave(features, prepare, probes, centered, scores):
    waiting = []
    for start in range(0, features, CHUNK):
        cols, first = slice(start, start + CHUNK), start == 0
        work = prepare(cols, first)
        share = -(-len(work) // max(len(waiting), 1))
        for i in range(0, len(work), share):
            if waiting:
                waiting.pop(0)()
            for step in work[i : i + share]:
                step()
        waiting += [
            functools.partial(add_products, cols, queries, probes, centered, scores, first)
            for queries in row_groups(probes.shape[0], BLOCK)
        ]
    for step in waiting:
        step()


def log_sum(squares, scores, queries):
    half = 0.5 * jnp.sum(squares[...], axis=1, keepdims=True)
    x = (scores[:, queries] - half) * (1 / TEMP)
    top = jnp.max(x, axis=0, keepdims=True)
    return jnp.log(jnp.sum(jnp.exp(x - top), axis=0, keepdims=True)) + top


def total_kernel(rows, total):
    total[...] = jnp.sum(rows[...].astype(jnp.float32), axis=0, keepdims=True)


def feature_total(rows, beside):
    in_vmem = pl.BlockSpec(memory_space=pltpu.VMEM)
    return pl.pallas_call(
        total_kernel,
        out_shape=jax.ShapeDtypeStruct((1, rows.shape[1]), jnp.float32),
        in_specs=[in_vmem],
        out_specs=in_vmem,
        compiler_params=pltpu.CompilerParams(vmem_limit_bytes=LIMIT),
        cost_estimate=pl.CostEstimate(
            flops=rows.size, bytes_accessed=4 * beside.size, transcendentals=0
        ),
    )(rows)


def ref_kernel(spans, queries, first_total, *refs):
    panel, (probes, mean, ref_log, centered, squares, scores) = refs[: len(spans)], refs[len(spans) :]
    groups = panel_groups(panel, spans)
    count, features = centered.shape

    def take_mean(cols):
        total = first_total[:, cols]
        for ref, rows, _ in groups:
            if ref is not panel[0]:
                total += jnp.sum(ref[rows, cols].astype(jnp.float32), axis=0, keepdims=True)
        mean[:, cols] = total * (1 / count) if count & (count - 1) == 0 else total / count

    def center_queries(rows, cols):
        probes[rows, cols] = center(queries[rows, cols], mean[:, cols])

    def prepare(cols, first):
        work = [functools.partial(take_mean, cols)]
        for group in groups:
            work.append(functools.partial(center_group, group, cols, mean, centered, squares, first))
        for rows in row_groups(probes.shape[0], GROUP):
            work.append(functools.partial(center_queries, rows, cols))
        return work

    interleave(features, prepare, probes, centered, scores)
    for block in row_groups(probes.shape[0], BLOCK):
        ref_log[:, block] = log_sum(squares, scores, block)


def gen_kernel(spans, ref_log, probes, mean, *refs):
    panel, (proof, centered, squares, scores) = refs[: len(spans)], refs[len(spans) :]
    groups = panel_groups(panel, spans)

    def prepare(cols, first):
        return [
            functools.partial(center_group, group, cols, mean, centered, squares, first)
            for group in groups
        ]

    interleave(centered.shape[1], prepare, probes, centered, scores)
    for block in row_groups(probes.shape[0], BLOCK):
        proof[:, block] = log_sum(squares, scores, block) - ref_log[:, block]


def call(kernel, before, pieces, count, out_shape):
    spans = [(low, high) for _, low, high in pieces]
    operands = [*before, *(array for array, _, _ in pieces)]
    rows, features = sum(high - low for low, high in spans), operands[-1].shape[1]
    in_vmem = pl.BlockSpec(memory_space=pltpu.VMEM)
    return pl.pallas_call(
        functools.partial(kernel, spans),
        out_shape=out_shape,
        in_specs=[in_vmem] * len(operands),
        out_specs=jax.tree.map(lambda _: in_vmem, out_shape),
        scratch_shapes=[
            pltpu.VMEM((rows, features), jnp.bfloat16),
            pltpu.VMEM((rows, LANES), jnp.float32),
            pltpu.VMEM((rows, count), jnp.float32),
        ],
        compiler_params=pltpu.CompilerParams(vmem_limit_bytes=LIMIT),
        cost_estimate=pl.CostEstimate(
            flops=2 * rows * count * features,
            bytes_accessed=2 * (rows + count) * features,
            transcendentals=rows * count,
        ),
    )(*operands)


def body(queries, gen_panel, ref_panel):
    panels = [ref_panel, gen_panel]
    (ref_pieces, gen_pieces), first_total = gather_panels(
        panels, lax.axis_size("samp"), functools.partial(feature_total, beside=queries)
    )
    count, features = queries.shape
    logs = jax.ShapeDtypeStruct((1, count), jnp.float32)
    probes, mean, ref_log = call(
        ref_kernel,
        [queries, first_total],
        ref_pieces,
        count,
        (
            jax.ShapeDtypeStruct((count, features), jnp.bfloat16),
            jax.ShapeDtypeStruct((1, features), jnp.float32),
            logs,
        ),
    )
    return call(gen_kernel, [ref_log, probes, mean], gen_pieces, count, logs).reshape(-1)


def solution(mesh):
    return jax.shard_map(
        body,
        mesh=mesh,
        in_specs=(
            P(("groups", "samp"), None),
            P(("groups", "samp"), None),
            P(("groups", "samp"), None),
        ),
        out_specs=P(("groups", "samp")),
        check_vma=False,
    )
```

```python
import functools

import jax
import jax.numpy as jnp
from jax import lax
from jax.experimental import pallas as pl
from jax.experimental.pallas import tpu as pltpu
from jax.sharding import PartitionSpec as P

TEMP = 64
LANES = 128
CHUNK = 1024
GROUP = 32
LIMIT = 40 * 2**20


def ring_of_chips(chips):
    return list(range(0, chips, 2)) + list(range(chips - 1 - chips % 2, 0, -2))


def ring_pairs(size):
    order = ring_of_chips(size // 2)
    pairs = []
    for place, chip in enumerate(order):
        after = order[(place + 1) % len(order)]
        before = order[place - 1]
        pairs.append((2 * chip, 2 * after))
        pairs.append((2 * chip + 1, 2 * before + 1))
    return pairs


def core_pairs(size):
    return [(i, i ^ 1) for i in range(size)]


def gather_panels(panels, size, on_first):
    twins, ring = core_pairs(size), ring_pairs(size)
    chips, rows = size // 2, panels[0].shape[0]

    def hop(block):
        return lax.ppermute(block, "samp", ring)

    def hand_over(block):
        return lax.ppermute(block, "samp", twins)

    steps = (chips - 1) // 2
    mine, other = list(panels), None
    pieces = [[] for _ in panels]
    fresh = [[] for _ in panels]
    for period in range(steps + 1):
        last = period == steps
        if last and period:
            other[0], extra = lax.optimization_barrier((other[0], extra))
        other = [hop(o) for o in other] if period else [hand_over(p) for p in panels]
        if not period:
            extra = on_first(other[0])
        arrived = [[] for _ in panels]
        if not last or chips % 2 == 0:
            mine = [hop(m) for m in mine]
            arrived = [[m] for m in mine]
        for i, o in enumerate(other):
            pieces[i] += [(a, 0, rows) for a in [o] + arrived[i]]
            fresh[i] += [o] + arrived[i]
        if last:
            for i in range(len(panels)):
                if fresh[i]:
                    block = hand_over(jnp.concatenate(fresh[i], axis=0))
                    pieces[i].append((block, 0, block.shape[0]))
        elif period and period < steps - 1:
            block, at = hand_over(jnp.concatenate([f for g in fresh for f in g], axis=0)), 0
            for i in range(len(panels)):
                upto = at + rows * len(fresh[i])
                pieces[i].append((block, at, upto))
                fresh[i], at = [], upto
    return pieces, extra


def row_groups(rows, step):
    return [slice(r, min(r + step, rows)) for r in range(0, rows, step)]


def panel_groups(refs, spans):
    groups, at = [], 0
    for ref, (low, high) in zip(refs, spans):
        for rows in row_groups(high - low, GROUP):
            size = rows.stop - rows.start
            groups.append((ref, slice(low + rows.start, low + rows.stop), slice(at, at + size)))
            at += size
    return groups


def center(rows, mean):
    return (rows.astype(jnp.float32) - mean).astype(jnp.bfloat16)


def add_squares(rows, cols, centered, squares, first):
    wide = jnp.square(centered[rows, cols].astype(jnp.float32))
    total = wide[:, :LANES]
    for lane in range(LANES, wide.shape[1], LANES):
        total += wide[:, lane : lane + LANES]
    squares[rows, :] = total if first else squares[rows, :] + total


def add_products(cols, probes, centered, scores, first):
    products = lax.dot_general(
        centered[:, cols], probes[:, cols], (((1,), (1,)), ((), ())),
        preferred_element_type=jnp.float32,
    )
    scores[...] = products if first else scores[...] + products


def log_sum(squares, scores):
    half = 0.5 * jnp.sum(squares[...], axis=1, keepdims=True)
    x = (scores[...] - half) * (1 / TEMP)
    top = jnp.max(x, axis=0, keepdims=True)
    return jnp.log(jnp.sum(jnp.exp(x - top), axis=0, keepdims=True)) + top


def total_kernel(rows, total):
    total[...] = jnp.sum(rows[...].astype(jnp.float32), axis=0, keepdims=True)


def feature_total(rows, beside):
    in_vmem = pl.BlockSpec(memory_space=pltpu.VMEM)
    return pl.pallas_call(
        total_kernel,
        out_shape=jax.ShapeDtypeStruct((1, rows.shape[1]), jnp.float32),
        in_specs=[in_vmem],
        out_specs=in_vmem,
        compiler_params=pltpu.CompilerParams(vmem_limit_bytes=LIMIT),
        cost_estimate=pl.CostEstimate(
            flops=rows.size, bytes_accessed=4 * beside.size, transcendentals=0
        ),
    )(rows)


def chunks(features):
    return [(slice(start, start + CHUNK), start == 0) for start in range(0, features, CHUNK)]


def ref_kernel(spans, queries, first_total, *refs):
    panel, (probes, mean, centered, scores) = refs[: len(spans)], refs[len(spans) :]
    groups = panel_groups(panel, spans)
    count, features = centered.shape
    for cols, first in chunks(features):
        total = first_total[:, cols]
        for ref, rows, _ in groups:
            if ref is not panel[0]:
                total += jnp.sum(ref[rows, cols].astype(jnp.float32), axis=0, keepdims=True)
        here = total / count
        mean[:, cols] = here
        for ref, rows, to in groups:
            centered[to, cols] = center(ref[rows, cols], here)
        for rows in row_groups(queries.shape[0], GROUP):
            probes[rows, cols] = center(queries[rows, cols], here)
        add_products(cols, probes, centered, scores, first)


def gen_kernel(spans, probes, mean, ref_centered, ref_scores, *refs):
    panel, (proof, centered, squares, scores, ref_squares) = refs[: len(spans)], refs[len(spans) :]
    groups = panel_groups(panel, spans)
    for cols, first in chunks(centered.shape[1]):
        for ref, rows, to in groups:
            centered[to, cols] = center(ref[rows, cols], mean[:, cols])
            add_squares(to, cols, centered, squares, first)
        add_products(cols, probes, centered, scores, first)
        for rows in row_groups(ref_centered.shape[0], GROUP):
            add_squares(rows, cols, ref_centered, ref_squares, first)
    ref_log = log_sum(ref_squares, ref_scores)
    proof[...] = log_sum(squares, scores) - ref_log


def call(kernel, before, pieces, count, out_shape, scratch):
    spans = [(low, high) for _, low, high in pieces]
    operands = [*before, *(array for array, _, _ in pieces)]
    rows, features = sum(high - low for low, high in spans), operands[-1].shape[1]
    in_vmem = pl.BlockSpec(memory_space=pltpu.VMEM)
    return pl.pallas_call(
        functools.partial(kernel, spans),
        out_shape=out_shape,
        in_specs=[in_vmem] * len(operands),
        out_specs=jax.tree.map(lambda _: in_vmem, out_shape),
        scratch_shapes=[pltpu.VMEM(s.shape, s.dtype) for s in scratch],
        compiler_params=pltpu.CompilerParams(vmem_limit_bytes=LIMIT),
        cost_estimate=pl.CostEstimate(
            flops=2 * rows * count * features,
            bytes_accessed=2 * (rows + count) * features,
            transcendentals=rows * count,
        ),
    )(*operands)


def body(queries, gen_panel, ref_panel):
    panels, size = [ref_panel, gen_panel], lax.axis_size("samp")
    (ref_pieces, gen_pieces), first_total = gather_panels(
        panels, size, functools.partial(feature_total, beside=queries)
    )
    count, features = queries.shape
    rows = size * ref_panel.shape[0]
    float32 = functools.partial(jax.ShapeDtypeStruct, dtype=jnp.float32)
    centered = jax.ShapeDtypeStruct((rows, features), jnp.bfloat16)
    squares, scores = float32((rows, LANES)), float32((rows, count))
    probes = jax.ShapeDtypeStruct((count, features), jnp.bfloat16)
    outputs = (probes, float32((1, features)), centered, scores)
    before = call(ref_kernel, [queries, first_total], ref_pieces, count, outputs, [])
    scratch = [centered, squares, scores, squares]
    return call(gen_kernel, before, gen_pieces, count, float32((1, count)), scratch).reshape(-1)


def solution(mesh):
    return jax.shard_map(
        body,
        mesh=mesh,
        in_specs=(
            P(("groups", "samp"), None),
            P(("groups", "samp"), None),
            P(("groups", "samp"), None),
        ),
        out_specs=P(("groups", "samp")),
        check_vma=False,
    )
```

```python
import functools

import jax
import jax.numpy as jnp
from jax import lax
from jax.experimental import pallas as pl
from jax.experimental.pallas import tpu as pltpu
from jax.sharding import PartitionSpec as P

TEMP = 64
LANES = 128
CHUNK = 1024
GROUP = 32
BLOCK = 256
LIMIT = 40 * 2**20


def ring_of_chips(chips):
    return list(range(0, chips, 2)) + list(range(chips - 1 - chips % 2, 0, -2))


def ring_pairs(size):
    order = ring_of_chips(size // 2)
    pairs = []
    for place, chip in enumerate(order):
        after = order[(place + 1) % len(order)]
        before = order[place - 1]
        pairs.append((2 * chip, 2 * after))
        pairs.append((2 * chip + 1, 2 * before + 1))
    return pairs


def core_pairs(size):
    return [(i, i ^ 1) for i in range(size)]


def gather_panels(panels, size, on_first):
    twins, ring = core_pairs(size), ring_pairs(size)
    chips, rows = size // 2, panels[0].shape[0]

    def hop(block):
        return lax.ppermute(block, "samp", ring)

    def hand_over(block):
        return lax.ppermute(block, "samp", twins)

    steps = (chips - 1) // 2
    mine, other = list(panels), None
    pieces = [[] for _ in panels]
    fresh = [[] for _ in panels]
    for period in range(steps + 1):
        last = period == steps
        if last and period:
            other[0], extra = lax.optimization_barrier((other[0], extra))
        other = [hop(o) for o in other] if period else [hand_over(p) for p in panels]
        if not period:
            extra = on_first(other[0])
        arrived = [[] for _ in panels]
        if not last or chips % 2 == 0:
            mine = [hop(m) for m in mine]
            arrived = [[m] for m in mine]
        for i, o in enumerate(other):
            pieces[i] += [(a, 0, rows) for a in [o] + arrived[i]]
            fresh[i] += [o] + arrived[i]
        if last:
            for i in range(len(panels)):
                if fresh[i]:
                    block = hand_over(jnp.concatenate(fresh[i], axis=0))
                    pieces[i].append((block, 0, block.shape[0]))
        elif period and period < steps - 1:
            block, at = hand_over(jnp.concatenate([f for g in fresh for f in g], axis=0)), 0
            for i in range(len(panels)):
                upto = at + rows * len(fresh[i])
                pieces[i].append((block, at, upto))
                fresh[i], at = [], upto
    return pieces, extra


def row_groups(rows, step):
    return [slice(r, min(r + step, rows)) for r in range(0, rows, step)]


def panel_groups(refs, spans):
    groups, at = [], 0
    for ref, (low, high) in zip(refs, spans):
        for rows in row_groups(high - low, GROUP):
            size = rows.stop - rows.start
            groups.append((ref, slice(low + rows.start, low + rows.stop), slice(at, at + size)))
            at += size
    return groups


def center(rows, mean):
    return (rows.astype(jnp.float32) - mean).astype(jnp.bfloat16)


def center_group(group, at, mean, centered, squares):
    ref, rows, here = group
    part = center(ref[rows, chunk(at)], mean[:, chunk(at)])
    centered[at][here, :] = part
    wide = jnp.square(part.astype(jnp.float32))
    total = wide[:, :LANES]
    for lane in range(LANES, wide.shape[1], LANES):
        total += wide[:, lane : lane + LANES]
    squares[here, :] = total if at == 0 else squares[here, :] + total


def add_products(at, queries, probes, centered, scores):
    products = lax.dot_general(
        centered[at][...], probes[at][queries, :], (((1,), (1,)), ((), ())),
        preferred_element_type=jnp.float32,
    )
    scores[:, queries] = products if at == 0 else scores[:, queries] + products


def chunk(at):
    return slice(at * CHUNK, (at + 1) * CHUNK)


def interleave(prepare, probes, centered, scores):
    waiting = []
    for at in range(len(centered)):
        work = prepare(at)
        share = -(-len(work) // max(len(waiting), 1))
        for i in range(0, len(work), share):
            if waiting:
                waiting.pop(0)()
            for step in work[i : i + share]:
                step()
        waiting += [
            functools.partial(add_products, at, queries, probes, centered, scores)
            for queries in row_groups(probes[at].shape[0], BLOCK)
        ]
    for step in waiting:
        step()


def log_sum(squares, scores, queries):
    half = 0.5 * jnp.sum(squares[...], axis=1, keepdims=True)
    x = (scores[:, queries] - half) * (1 / TEMP)
    top = jnp.max(x, axis=0, keepdims=True)
    return jnp.log(jnp.sum(jnp.exp(x - top), axis=0, keepdims=True)) + top


def total_kernel(rows, total):
    total[...] = jnp.sum(rows[...].astype(jnp.float32), axis=0, keepdims=True)


def feature_total(rows, beside):
    in_vmem = pl.BlockSpec(memory_space=pltpu.VMEM)
    return pl.pallas_call(
        total_kernel,
        out_shape=jax.ShapeDtypeStruct((1, rows.shape[1]), jnp.float32),
        in_specs=[in_vmem],
        out_specs=in_vmem,
        compiler_params=pltpu.CompilerParams(vmem_limit_bytes=LIMIT),
        cost_estimate=pl.CostEstimate(
            flops=rows.size, bytes_accessed=4 * beside.size, transcendentals=0
        ),
    )(rows)


def split(refs, *counts):
    runs = []
    for count in counts:
        runs.append(refs[:count])
        refs = refs[count:]
    return *runs, refs


def ref_kernel(spans, parts, queries, first_total, *refs):
    panel, probes, centered, (mean, ref_log, squares, scores) = arrange(refs, spans, parts)
    groups = panel_groups(panel, spans)
    count = scores.shape[0]

    def take_mean(at):
        cols = chunk(at)
        total = first_total[:, cols]
        for ref, rows, _ in groups:
            if ref is not panel[0]:
                total += jnp.sum(ref[rows, cols].astype(jnp.float32), axis=0, keepdims=True)
        mean[:, cols] = total / count

    def center_queries(rows, at):
        probes[at][rows, :] = center(queries[rows, chunk(at)], mean[:, chunk(at)])

    def prepare(at):
        work = [functools.partial(take_mean, at)]
        for group in groups:
            work.append(functools.partial(center_group, group, at, mean, centered, squares))
        for rows in row_groups(queries.shape[0], GROUP):
            work.append(functools.partial(center_queries, rows, at))
        return work

    interleave(prepare, probes, centered, scores)
    for block in row_groups(queries.shape[0], BLOCK):
        ref_log[:, block] = log_sum(squares, scores, block)


def arrange(refs, spans, parts):
    panel, probes, (mean, log), centered, rest = split(refs, len(spans), parts, 2, parts)
    return panel, probes, centered, (mean, log, *rest)


def gen_kernel(spans, parts, *refs):
    probes, (mean, ref_log), panel, (proof,), centered, (squares, scores) = split(
        refs, parts, 2, len(spans), 1, parts
    )
    groups = panel_groups(panel, spans)

    def prepare(at):
        return [
            functools.partial(center_group, group, at, mean, centered, squares)
            for group in groups
        ]

    interleave(prepare, probes, centered, scores)
    for block in row_groups(probes[0].shape[0], BLOCK):
        proof[:, block] = log_sum(squares, scores, block) - ref_log[:, block]


def call(kernel, before, pieces, count, out_shape):
    spans = [(low, high) for _, low, high in pieces]
    operands = [*before, *(array for array, _, _ in pieces)]
    rows, features = sum(high - low for low, high in spans), operands[-1].shape[1]
    parts = features // CHUNK
    in_vmem = pl.BlockSpec(memory_space=pltpu.VMEM)
    return pl.pallas_call(
        functools.partial(kernel, spans, parts),
        out_shape=out_shape,
        in_specs=[in_vmem] * len(operands),
        out_specs=jax.tree.map(lambda _: in_vmem, out_shape),
        scratch_shapes=[pltpu.VMEM((rows, CHUNK), jnp.bfloat16)] * parts
        + [pltpu.VMEM((rows, LANES), jnp.float32), pltpu.VMEM((rows, count), jnp.float32)],
        compiler_params=pltpu.CompilerParams(vmem_limit_bytes=LIMIT),
        cost_estimate=pl.CostEstimate(
            flops=2 * rows * count * features,
            bytes_accessed=2 * (rows + count) * features,
            transcendentals=rows * count,
        ),
    )(*operands)


def body(queries, gen_panel, ref_panel):
    panels = [ref_panel, gen_panel]
    (ref_pieces, gen_pieces), first_total = gather_panels(
        panels, lax.axis_size("samp"), functools.partial(feature_total, beside=queries)
    )
    count, features = queries.shape
    logs = jax.ShapeDtypeStruct((1, count), jnp.float32)
    probes = jax.ShapeDtypeStruct((count, CHUNK), jnp.bfloat16)
    mean = jax.ShapeDtypeStruct((1, features), jnp.float32)
    outputs = (*[probes] * (features // CHUNK), mean, logs)
    before = call(ref_kernel, [queries, first_total], ref_pieces, count, outputs)
    return call(gen_kernel, before, gen_pieces, count, logs).reshape(-1)


def solution(mesh):
    return jax.shard_map(
        body,
        mesh=mesh,
        in_specs=(
            P(("groups", "samp"), None),
            P(("groups", "samp"), None),
            P(("groups", "samp"), None),
        ),
        out_specs=P(("groups", "samp")),
        check_vma=False,
    )
```

```python
import functools

import jax
import jax.numpy as jnp
from jax import lax
from jax.experimental import pallas as pl
from jax.experimental.pallas import tpu as pltpu
from jax.sharding import PartitionSpec as P

TEMP = 64
LANES = 128
CHUNK = 256
GROUP = 32
BLOCK = 256
LIMIT = 40 * 2**20


def ring_of_chips(chips):
    return list(range(0, chips, 2)) + list(range(chips - 1 - chips % 2, 0, -2))


def ring_pairs(size):
    order = ring_of_chips(size // 2)
    pairs = []
    for place, chip in enumerate(order):
        after = order[(place + 1) % len(order)]
        before = order[place - 1]
        pairs.append((2 * chip, 2 * after))
        pairs.append((2 * chip + 1, 2 * before + 1))
    return pairs


def core_pairs(size):
    return [(i, i ^ 1) for i in range(size)]


def gather_panels(panels, size, on_first):
    twins, ring = core_pairs(size), ring_pairs(size)
    chips, rows = size // 2, panels[0].shape[0]

    def hop(block):
        return lax.ppermute(block, "samp", ring)

    def hand_over(block):
        return lax.ppermute(block, "samp", twins)

    steps = (chips - 1) // 2
    mine, other = list(panels), None
    pieces = [[] for _ in panels]
    fresh = [[] for _ in panels]
    for period in range(steps + 1):
        last = period == steps
        if last and period:
            other[0], extra = lax.optimization_barrier((other[0], extra))
        other = [hop(o) for o in other] if period else [hand_over(p) for p in panels]
        if not period:
            extra = on_first(other[0])
        arrived = [[] for _ in panels]
        if not last or chips % 2 == 0:
            mine = [hop(m) for m in mine]
            arrived = [[m] for m in mine]
        for i, o in enumerate(other):
            pieces[i] += [(a, 0, rows) for a in [o] + arrived[i]]
            fresh[i] += [o] + arrived[i]
        if last:
            for i in range(len(panels)):
                if fresh[i]:
                    block = hand_over(jnp.concatenate(fresh[i], axis=0))
                    pieces[i].append((block, 0, block.shape[0]))
        elif period and period < steps - 1:
            block, at = hand_over(jnp.concatenate([f for g in fresh for f in g], axis=0)), 0
            for i in range(len(panels)):
                upto = at + rows * len(fresh[i])
                pieces[i].append((block, at, upto))
                fresh[i], at = [], upto
    return pieces, extra


def row_groups(rows, step):
    return [slice(r, min(r + step, rows)) for r in range(0, rows, step)]


def panel_groups(refs, spans):
    groups, at = [], 0
    for ref, (low, high) in zip(refs, spans):
        for rows in row_groups(high - low, GROUP):
            size = rows.stop - rows.start
            groups.append((ref, slice(low + rows.start, low + rows.stop), slice(at, at + size)))
            at += size
    return groups


def center(rows, mean):
    return (rows.astype(jnp.float32) - mean).astype(jnp.bfloat16)


def center_group(group, at, mean, centered, squares):
    ref, rows, here = group
    part = center(ref[rows, chunk(at)], mean[:, chunk(at)])
    centered[at][here, :] = part
    wide = jnp.square(part.astype(jnp.float32))
    total = wide[:, :LANES]
    for lane in range(LANES, wide.shape[1], LANES):
        total += wide[:, lane : lane + LANES]
    squares[here, :] = total if at == 0 else squares[here, :] + total


def add_products(at, queries, probes, centered, scores):
    products = lax.dot_general(
        centered[at][...], probes[at][queries, :], (((1,), (1,)), ((), ())),
        preferred_element_type=jnp.float32,
    )
    scores[:, queries] = products if at == 0 else scores[:, queries] + products


def chunk(at):
    return slice(at * CHUNK, (at + 1) * CHUNK)


def interleave(prepare, probes, centered, scores):
    waiting = []
    for at in range(len(centered)):
        work = prepare(at)
        share = -(-len(work) // max(len(waiting), 1))
        for i in range(0, len(work), share):
            if waiting:
                waiting.pop(0)()
            for step in work[i : i + share]:
                step()
        waiting += [
            functools.partial(add_products, at, queries, probes, centered, scores)
            for queries in row_groups(probes[at].shape[0], BLOCK)
        ]
    for step in waiting:
        step()


def log_sum(squares, scores, queries):
    half = 0.5 * jnp.sum(squares[...], axis=1, keepdims=True)
    x = (scores[:, queries] - half) * (1 / TEMP)
    top = jnp.max(x, axis=0, keepdims=True)
    return jnp.log(jnp.sum(jnp.exp(x - top), axis=0, keepdims=True)) + top


def total_kernel(rows, total):
    total[...] = jnp.sum(rows[...].astype(jnp.float32), axis=0, keepdims=True)


def feature_total(rows, beside):
    in_vmem = pl.BlockSpec(memory_space=pltpu.VMEM)
    return pl.pallas_call(
        total_kernel,
        out_shape=jax.ShapeDtypeStruct((1, rows.shape[1]), jnp.float32),
        in_specs=[in_vmem],
        out_specs=in_vmem,
        compiler_params=pltpu.CompilerParams(vmem_limit_bytes=LIMIT),
        cost_estimate=pl.CostEstimate(
            flops=rows.size, bytes_accessed=4 * beside.size, transcendentals=0
        ),
    )(rows)


def split(refs, *counts):
    runs = []
    for count in counts:
        runs.append(refs[:count])
        refs = refs[count:]
    return *runs, refs


def ref_kernel(spans, parts, queries, first_total, *refs):
    panel, probes, centered, (mean, ref_log, squares, scores) = arrange(refs, spans, parts)
    groups = panel_groups(panel, spans)
    count = scores.shape[0]

    def take_mean(at):
        cols = chunk(at)
        total = first_total[:, cols]
        for ref, rows, _ in groups:
            if ref is not panel[0]:
                total += jnp.sum(ref[rows, cols].astype(jnp.float32), axis=0, keepdims=True)
        mean[:, cols] = total / count

    def center_queries(rows, at):
        probes[at][rows, :] = center(queries[rows, chunk(at)], mean[:, chunk(at)])

    def prepare(at):
        work = [functools.partial(take_mean, at)]
        for group in groups:
            work.append(functools.partial(center_group, group, at, mean, centered, squares))
        for rows in row_groups(queries.shape[0], GROUP):
            work.append(functools.partial(center_queries, rows, at))
        return work

    interleave(prepare, probes, centered, scores)
    for block in row_groups(queries.shape[0], BLOCK):
        ref_log[:, block] = log_sum(squares, scores, block)


def arrange(refs, spans, parts):
    panel, probes, (mean, log), centered, rest = split(refs, len(spans), parts, 2, parts)
    return panel, probes, centered, (mean, log, *rest)


def gen_kernel(spans, parts, *refs):
    probes, (mean, ref_log), panel, (proof,), centered, (squares, scores) = split(
        refs, parts, 2, len(spans), 1, parts
    )
    groups = panel_groups(panel, spans)

    def prepare(at):
        return [
            functools.partial(center_group, group, at, mean, centered, squares)
            for group in groups
        ]

    interleave(prepare, probes, centered, scores)
    for block in row_groups(probes[0].shape[0], BLOCK):
        proof[:, block] = log_sum(squares, scores, block) - ref_log[:, block]


def call(kernel, before, pieces, count, out_shape):
    spans = [(low, high) for _, low, high in pieces]
    operands = [*before, *(array for array, _, _ in pieces)]
    rows, features = sum(high - low for low, high in spans), operands[-1].shape[1]
    parts = features // CHUNK
    in_vmem = pl.BlockSpec(memory_space=pltpu.VMEM)
    return pl.pallas_call(
        functools.partial(kernel, spans, parts),
        out_shape=out_shape,
        in_specs=[in_vmem] * len(operands),
        out_specs=jax.tree.map(lambda _: in_vmem, out_shape),
        scratch_shapes=[pltpu.VMEM((rows, CHUNK), jnp.bfloat16)] * parts
        + [pltpu.VMEM((rows, LANES), jnp.float32), pltpu.VMEM((rows, count), jnp.float32)],
        compiler_params=pltpu.CompilerParams(vmem_limit_bytes=LIMIT),
        cost_estimate=pl.CostEstimate(
            flops=2 * rows * count * features,
            bytes_accessed=2 * (rows + count) * features,
            transcendentals=rows * count,
        ),
    )(*operands)


def body(queries, gen_panel, ref_panel):
    panels = [ref_panel, gen_panel]
    (ref_pieces, gen_pieces), first_total = gather_panels(
        panels, lax.axis_size("samp"), functools.partial(feature_total, beside=queries)
    )
    count, features = queries.shape
    logs = jax.ShapeDtypeStruct((1, count), jnp.float32)
    probes = jax.ShapeDtypeStruct((count, CHUNK), jnp.bfloat16)
    mean = jax.ShapeDtypeStruct((1, features), jnp.float32)
    outputs = (*[probes] * (features // CHUNK), mean, logs)
    before = call(ref_kernel, [queries, first_total], ref_pieces, count, outputs)
    return call(gen_kernel, before, gen_pieces, count, logs).reshape(-1)


def solution(mesh):
    return jax.shard_map(
        body,
        mesh=mesh,
        in_specs=(
            P(("groups", "samp"), None),
            P(("groups", "samp"), None),
            P(("groups", "samp"), None),
        ),
        out_specs=P(("groups", "samp")),
        check_vma=False,
    )
```

```python
import functools

import jax
import jax.numpy as jnp
from jax import lax
from jax.experimental import pallas as pl
from jax.experimental.pallas import tpu as pltpu
from jax.sharding import PartitionSpec as P

TEMP = 64
LANES = 128
CHUNK = 1024
GROUP = 32
BLOCK = 256
LIMIT = 40 * 2**20


def ring_of_chips(chips):
    return list(range(0, chips, 2)) + list(range(chips - 1 - chips % 2, 0, -2))


def ring_pairs(size):
    order = ring_of_chips(size // 2)
    pairs = []
    for place, chip in enumerate(order):
        after = order[(place + 1) % len(order)]
        before = order[place - 1]
        pairs.append((2 * chip, 2 * after))
        pairs.append((2 * chip + 1, 2 * before + 1))
    return pairs


def core_pairs(size):
    return [(i, i ^ 1) for i in range(size)]


def gather_panels(panels, size, on_first, on_next):
    twins, ring = core_pairs(size), ring_pairs(size)
    chips, rows = size // 2, panels[0].shape[0]

    def hop(block):
        return lax.ppermute(block, "samp", ring)

    def hand_over(block):
        return lax.ppermute(block, "samp", twins)

    steps = (chips - 1) // 2
    mine, other = list(panels), None
    pieces = [[] for _ in panels]
    fresh = [[] for _ in panels]
    for period in range(steps + 1):
        last = period == steps
        if last and period:
            other[0], extra = lax.optimization_barrier((other[0], extra))
        other = [hop(o) for o in other] if period else [hand_over(p) for p in panels]
        if not period:
            extra = on_first(other[0])
        arrived = [[] for _ in panels]
        if not last or chips % 2 == 0:
            mine = [hop(m) for m in mine]
            arrived = [[m] for m in mine]
        for i, o in enumerate(other):
            pieces[i] += [(a, 0, rows) for a in [o] + arrived[i]]
            fresh[i] += [o] + arrived[i]
        if last:
            for i in range(len(panels)):
                if fresh[i]:
                    block = jnp.concatenate(fresh[i], axis=0)
                    if i == 0:
                        now = [k for k, piece in enumerate(pieces[0]) if k and piece[0].shape[0] == rows]
                        late = [k for k in range(1, len(pieces[0]) + 1) if k not in now]
                        total = on_next([pieces[0][k] for k in now])
                        block, total = lax.optimization_barrier((block, total))
                    block = hand_over(block)
                    pieces[i].append((block, 0, block.shape[0]))
        elif period and period < steps - 1:
            block, at = hand_over(jnp.concatenate([f for g in fresh for f in g], axis=0)), 0
            for i in range(len(panels)):
                upto = at + rows * len(fresh[i])
                pieces[i].append((block, at, upto))
                fresh[i], at = [], upto
    return pieces, (extra, total), late


def row_groups(rows, step):
    return [slice(r, min(r + step, rows)) for r in range(0, rows, step)]


def panel_groups(refs, spans):
    groups, at = [], 0
    for ref, (low, high) in zip(refs, spans):
        for rows in row_groups(high - low, GROUP):
            size = rows.stop - rows.start
            groups.append((ref, slice(low + rows.start, low + rows.stop), slice(at, at + size)))
            at += size
    return groups


def center(rows, mean):
    return (rows.astype(jnp.float32) - mean).astype(jnp.bfloat16)


def center_group(group, cols, mean, centered, squares, first):
    ref, rows, here = group
    part = center(ref[rows, cols], mean[:, cols])
    centered[here, cols] = part
    wide = jnp.square(part.astype(jnp.float32))
    total = wide[:, :LANES]
    for lane in range(LANES, wide.shape[1], LANES):
        total += wide[:, lane : lane + LANES]
    squares[here, :] = total if first else squares[here, :] + total


def add_products(cols, queries, probes, centered, scores, first):
    products = lax.dot_general(
        centered[:, cols], probes[queries, cols], (((1,), (1,)), ((), ())),
        preferred_element_type=jnp.float32,
    )
    scores[:, queries] = products if first else scores[:, queries] + products


def interleave(features, prepare, probes, centered, scores):
    waiting = []
    for start in range(0, features, CHUNK):
        cols, first = slice(start, start + CHUNK), start == 0
        work = prepare(cols, first)
        share = -(-len(work) // max(len(waiting), 1))
        for i in range(0, len(work), share):
            if waiting:
                waiting.pop(0)()
            for step in work[i : i + share]:
                step()
        waiting += [
            functools.partial(add_products, cols, queries, probes, centered, scores, first)
            for queries in row_groups(probes.shape[0], BLOCK)
        ]
    for step in waiting:
        step()


def log_sum(squares, scores, queries):
    half = 0.5 * jnp.sum(squares[...], axis=1, keepdims=True)
    x = (scores[:, queries] - half) * (1 / TEMP)
    top = jnp.max(x, axis=0, keepdims=True)
    return jnp.log(jnp.sum(jnp.exp(x - top), axis=0, keepdims=True)) + top


def total_kernel(spans, *refs):
    *panel, total = refs
    for start in range(0, total.shape[1], CHUNK):
        cols = slice(start, start + CHUNK)
        sums = [
            jnp.sum(ref[low:high, cols].astype(jnp.float32), axis=0, keepdims=True)
            for ref, (low, high) in zip(panel, spans)
        ]
        total[:, cols] = functools.reduce(jnp.add, sums)


def feature_total(pieces, cost):
    in_vmem = pl.BlockSpec(memory_space=pltpu.VMEM)
    spans = [(low, high) for _, low, high in pieces]
    arrays = [array for array, _, _ in pieces]
    return pl.pallas_call(
        functools.partial(total_kernel, spans),
        out_shape=jax.ShapeDtypeStruct((1, arrays[0].shape[1]), jnp.float32),
        in_specs=[in_vmem] * len(arrays),
        out_specs=in_vmem,
        compiler_params=pltpu.CompilerParams(vmem_limit_bytes=LIMIT),
        cost_estimate=pl.CostEstimate(flops=0, bytes_accessed=cost, transcendentals=0),
    )(*arrays)


def ref_kernel(late, spans, queries, *refs):
    totals, refs = refs[:2], refs[2:]
    panel, (probes, mean, ref_log, centered, squares, scores) = refs[: len(spans)], refs[len(spans) :]
    groups = panel_groups(panel, spans)
    count, features = centered.shape
    for start in range(0, features, CHUNK):
        cols = slice(start, start + CHUNK)
        total = totals[0][:, cols] + totals[1][:, cols]
        for k in late:
            low, high = spans[k]
            total += jnp.sum(panel[k][low:high, cols].astype(jnp.float32), axis=0, keepdims=True)
        mean[:, cols] = total / count

    def center_queries(rows, cols):
        probes[rows, cols] = center(queries[rows, cols], mean[:, cols])

    def prepare(cols, first):
        work = []
        for group in groups:
            work.append(functools.partial(center_group, group, cols, mean, centered, squares, first))
        for rows in row_groups(probes.shape[0], GROUP):
            work.append(functools.partial(center_queries, rows, cols))
        return work

    interleave(features, prepare, probes, centered, scores)
    for block in row_groups(probes.shape[0], BLOCK):
        ref_log[:, block] = log_sum(squares, scores, block)


def gen_kernel(spans, ref_log, probes, mean, *refs):
    panel, (proof, centered, squares, scores) = refs[: len(spans)], refs[len(spans) :]
    groups = panel_groups(panel, spans)

    def prepare(cols, first):
        return [
            functools.partial(center_group, group, cols, mean, centered, squares, first)
            for group in groups
        ]

    interleave(centered.shape[1], prepare, probes, centered, scores)
    for block in row_groups(probes.shape[0], BLOCK):
        proof[:, block] = log_sum(squares, scores, block) - ref_log[:, block]


def call(kernel, before, pieces, count, out_shape):
    spans = [(low, high) for _, low, high in pieces]
    operands = [*before, *(array for array, _, _ in pieces)]
    rows, features = sum(high - low for low, high in spans), operands[-1].shape[1]
    in_vmem = pl.BlockSpec(memory_space=pltpu.VMEM)
    return pl.pallas_call(
        functools.partial(kernel, spans),
        out_shape=out_shape,
        in_specs=[in_vmem] * len(operands),
        out_specs=jax.tree.map(lambda _: in_vmem, out_shape),
        scratch_shapes=[
            pltpu.VMEM((rows, features), jnp.bfloat16),
            pltpu.VMEM((rows, LANES), jnp.float32),
            pltpu.VMEM((rows, count), jnp.float32),
        ],
        compiler_params=pltpu.CompilerParams(vmem_limit_bytes=LIMIT),
        cost_estimate=pl.CostEstimate(
            flops=2 * rows * count * features,
            bytes_accessed=2 * (rows + count) * features,
            transcendentals=rows * count,
        ),
    )(*operands)


def body(queries, gen_panel, ref_panel):
    panels = [ref_panel, gen_panel]
    (ref_pieces, gen_pieces), totals, late = gather_panels(
        panels,
        lax.axis_size("samp"),
        lambda rows: feature_total([(rows, 0, rows.shape[0])], 4 * queries.size),
        lambda pieces: feature_total(pieces, 0),
    )
    count, features = queries.shape
    logs = jax.ShapeDtypeStruct((1, count), jnp.float32)
    probes, mean, ref_log = call(
        functools.partial(ref_kernel, late),
        [queries, *totals],
        ref_pieces,
        count,
        (
            jax.ShapeDtypeStruct((count, features), jnp.bfloat16),
            jax.ShapeDtypeStruct((1, features), jnp.float32),
            logs,
        ),
    )
    return call(gen_kernel, [ref_log, probes, mean], gen_pieces, count, logs).reshape(-1)


def solution(mesh):
    return jax.shard_map(
        body,
        mesh=mesh,
        in_specs=(
            P(("groups", "samp"), None),
            P(("groups", "samp"), None),
            P(("groups", "samp"), None),
        ),
        out_specs=P(("groups", "samp")),
        check_vma=False,
    )
```

```python
import functools

import jax
import jax.numpy as jnp
from jax import lax
from jax.experimental import pallas as pl
from jax.experimental.pallas import tpu as pltpu
from jax.sharding import PartitionSpec as P

TEMP = 64
LANES = 128
CHUNK = 1024
GROUP = 64
BLOCK = 256
LIMIT = 40 * 2**20


def ring_of_chips(chips):
    return list(range(0, chips, 2)) + list(range(chips - 1 - chips % 2, 0, -2))


def ring_pairs(size):
    order = ring_of_chips(size // 2)
    pairs = []
    for place, chip in enumerate(order):
        after = order[(place + 1) % len(order)]
        before = order[place - 1]
        pairs.append((2 * chip, 2 * after))
        pairs.append((2 * chip + 1, 2 * before + 1))
    return pairs


def core_pairs(size):
    return [(i, i ^ 1) for i in range(size)]


def gather_panels(panels, size, on_first, on_next):
    twins, ring = core_pairs(size), ring_pairs(size)
    chips, rows = size // 2, panels[0].shape[0]

    def hop(block):
        return lax.ppermute(block, "samp", ring)

    def hand_over(block):
        return lax.ppermute(block, "samp", twins)

    steps = (chips - 1) // 2
    mine, other = list(panels), None
    pieces = [[] for _ in panels]
    fresh = [[] for _ in panels]
    for period in range(steps + 1):
        last = period == steps
        if last and period:
            other[0], extra = lax.optimization_barrier((other[0], extra))
        other = [hop(o) for o in other] if period else [hand_over(p) for p in panels]
        if not period:
            extra = on_first(other[0])
        arrived = [[] for _ in panels]
        if not last or chips % 2 == 0:
            mine = [hop(m) for m in mine]
            arrived = [[m] for m in mine]
        for i, o in enumerate(other):
            pieces[i] += [(a, 0, rows) for a in [o] + arrived[i]]
            fresh[i] += [o] + arrived[i]
        if last:
            for i in range(len(panels)):
                if fresh[i]:
                    block = jnp.concatenate(fresh[i], axis=0)
                    if i == 0:
                        now = [k for k, piece in enumerate(pieces[0]) if k and piece[0].shape[0] == rows]
                        late = [k for k in range(1, len(pieces[0]) + 1) if k not in now]
                        total = on_next([pieces[0][k] for k in now])
                        block, total = lax.optimization_barrier((block, total))
                    block = hand_over(block)
                    pieces[i].append((block, 0, block.shape[0]))
        elif period and period < steps - 1:
            block, at = hand_over(jnp.concatenate([f for g in fresh for f in g], axis=0)), 0
            for i in range(len(panels)):
                upto = at + rows * len(fresh[i])
                pieces[i].append((block, at, upto))
                fresh[i], at = [], upto
    return pieces, (extra, total), late


def row_groups(rows, step):
    return [slice(r, min(r + step, rows)) for r in range(0, rows, step)]


def panel_groups(refs, spans):
    groups, at = [], 0
    for ref, (low, high) in zip(refs, spans):
        for rows in row_groups(high - low, GROUP):
            size = rows.stop - rows.start
            groups.append((ref, slice(low + rows.start, low + rows.stop), slice(at, at + size)))
            at += size
    return groups


def center(rows, mean):
    return (rows.astype(jnp.float32) - mean).astype(jnp.bfloat16)


def center_group(group, cols, mean, centered, squares, first):
    ref, rows, here = group
    part = center(ref[rows, cols], mean[:, cols])
    centered[here, cols] = part
    wide = jnp.square(part.astype(jnp.float32))
    total = wide[:, :LANES]
    for lane in range(LANES, wide.shape[1], LANES):
        total += wide[:, lane : lane + LANES]
    squares[here, :] = total if first else squares[here, :] + total


def add_products(cols, queries, probes, centered, scores, first):
    products = lax.dot_general(
        centered[:, cols], probes[queries, cols], (((1,), (1,)), ((), ())),
        preferred_element_type=jnp.float32,
    )
    scores[:, queries] = products if first else scores[:, queries] + products


def interleave(features, prepare, probes, centered, scores):
    waiting = []
    for start in range(0, features, CHUNK):
        cols, first = slice(start, start + CHUNK), start == 0
        work = prepare(cols, first)
        share = -(-len(work) // max(len(waiting), 1))
        for i in range(0, len(work), share):
            if waiting:
                waiting.pop(0)()
            for step in work[i : i + share]:
                step()
        waiting += [
            functools.partial(add_products, cols, queries, probes, centered, scores, first)
            for queries in row_groups(probes.shape[0], BLOCK)
        ]
    for step in waiting:
        step()


def log_sum(squares, scores, queries):
    half = 0.5 * jnp.sum(squares[...], axis=1, keepdims=True)
    x = (scores[:, queries] - half) * (1 / TEMP)
    top = jnp.max(x, axis=0, keepdims=True)
    return jnp.log(jnp.sum(jnp.exp(x - top), axis=0, keepdims=True)) + top


def total_kernel(spans, *refs):
    *panel, total = refs
    for start in range(0, total.shape[1], CHUNK):
        cols = slice(start, start + CHUNK)
        sums = [
            jnp.sum(ref[low:high, cols].astype(jnp.float32), axis=0, keepdims=True)
            for ref, (low, high) in zip(panel, spans)
        ]
        total[:, cols] = functools.reduce(jnp.add, sums)


def feature_total(pieces, cost):
    in_vmem = pl.BlockSpec(memory_space=pltpu.VMEM)
    spans = [(low, high) for _, low, high in pieces]
    arrays = [array for array, _, _ in pieces]
    return pl.pallas_call(
        functools.partial(total_kernel, spans),
        out_shape=jax.ShapeDtypeStruct((1, arrays[0].shape[1]), jnp.float32),
        in_specs=[in_vmem] * len(arrays),
        out_specs=in_vmem,
        compiler_params=pltpu.CompilerParams(vmem_limit_bytes=LIMIT),
        cost_estimate=pl.CostEstimate(flops=0, bytes_accessed=cost, transcendentals=0),
    )(*arrays)


def ref_kernel(late, spans, queries, *refs):
    totals, refs = refs[:2], refs[2:]
    panel, (probes, mean, ref_log, centered, squares, scores) = refs[: len(spans)], refs[len(spans) :]
    groups = panel_groups(panel, spans)
    count, features = centered.shape
    for start in range(0, features, CHUNK):
        cols = slice(start, start + CHUNK)
        total = totals[0][:, cols] + totals[1][:, cols]
        for k in late:
            low, high = spans[k]
            total += jnp.sum(panel[k][low:high, cols].astype(jnp.float32), axis=0, keepdims=True)
        mean[:, cols] = total / count

    def center_queries(rows, cols):
        probes[rows, cols] = center(queries[rows, cols], mean[:, cols])

    def prepare(cols, first):
        work = []
        for group in groups:
            work.append(functools.partial(center_group, group, cols, mean, centered, squares, first))
        for rows in row_groups(probes.shape[0], GROUP):
            work.append(functools.partial(center_queries, rows, cols))
        return work

    interleave(features, prepare, probes, centered, scores)
    for block in row_groups(probes.shape[0], BLOCK):
        ref_log[:, block] = log_sum(squares, scores, block)


def gen_kernel(spans, ref_log, probes, mean, *refs):
    panel, (proof, centered, squares, scores) = refs[: len(spans)], refs[len(spans) :]
    groups = panel_groups(panel, spans)

    def prepare(cols, first):
        return [
            functools.partial(center_group, group, cols, mean, centered, squares, first)
            for group in groups
        ]

    interleave(centered.shape[1], prepare, probes, centered, scores)
    for block in row_groups(probes.shape[0], BLOCK):
        proof[:, block] = log_sum(squares, scores, block) - ref_log[:, block]


def call(kernel, before, pieces, count, out_shape):
    spans = [(low, high) for _, low, high in pieces]
    operands = [*before, *(array for array, _, _ in pieces)]
    rows, features = sum(high - low for low, high in spans), operands[-1].shape[1]
    in_vmem = pl.BlockSpec(memory_space=pltpu.VMEM)
    return pl.pallas_call(
        functools.partial(kernel, spans),
        out_shape=out_shape,
        in_specs=[in_vmem] * len(operands),
        out_specs=jax.tree.map(lambda _: in_vmem, out_shape),
        scratch_shapes=[
            pltpu.VMEM((rows, features), jnp.bfloat16),
            pltpu.VMEM((rows, LANES), jnp.float32),
            pltpu.VMEM((rows, count), jnp.float32),
        ],
        compiler_params=pltpu.CompilerParams(vmem_limit_bytes=LIMIT),
        cost_estimate=pl.CostEstimate(
            flops=2 * rows * count * features,
            bytes_accessed=2 * (rows + count) * features,
            transcendentals=rows * count,
        ),
    )(*operands)


def body(queries, gen_panel, ref_panel):
    panels = [ref_panel, gen_panel]
    (ref_pieces, gen_pieces), totals, late = gather_panels(
        panels,
        lax.axis_size("samp"),
        lambda rows: feature_total([(rows, 0, rows.shape[0])], 4 * queries.size),
        lambda pieces: feature_total(pieces, 0),
    )
    count, features = queries.shape
    logs = jax.ShapeDtypeStruct((1, count), jnp.float32)
    probes, mean, ref_log = call(
        functools.partial(ref_kernel, late),
        [queries, *totals],
        ref_pieces,
        count,
        (
            jax.ShapeDtypeStruct((count, features), jnp.bfloat16),
            jax.ShapeDtypeStruct((1, features), jnp.float32),
            logs,
        ),
    )
    return call(gen_kernel, [ref_log, probes, mean], gen_pieces, count, logs).reshape(-1)


def solution(mesh):
    return jax.shard_map(
        body,
        mesh=mesh,
        in_specs=(
            P(("groups", "samp"), None),
            P(("groups", "samp"), None),
            P(("groups", "samp"), None),
        ),
        out_specs=P(("groups", "samp")),
        check_vma=False,
    )
```

```python
import functools

import jax
import jax.numpy as jnp
from jax import lax
from jax.experimental import pallas as pl
from jax.experimental.pallas import tpu as pltpu
from jax.sharding import PartitionSpec as P

TEMP = 64
LANES = 128
CHUNK = 1024
GROUP = 32
BLOCK = 256
TURN = 256
LIMIT = 40 * 2**20


def ring_of_chips(chips):
    return list(range(0, chips, 2)) + list(range(chips - 1 - chips % 2, 0, -2))


def ring_pairs(size):
    order = ring_of_chips(size // 2)
    pairs = []
    for place, chip in enumerate(order):
        after = order[(place + 1) % len(order)]
        before = order[place - 1]
        pairs.append((2 * chip, 2 * after))
        pairs.append((2 * chip + 1, 2 * before + 1))
    return pairs


def core_pairs(size):
    return [(i, i ^ 1) for i in range(size)]


def gather_panels(panels, size, on_first, on_next):
    twins, ring = core_pairs(size), ring_pairs(size)
    chips, rows = size // 2, panels[0].shape[0]

    def hop(block):
        return lax.ppermute(block, "samp", ring)

    def hand_over(block):
        return lax.ppermute(block, "samp", twins)

    steps = (chips - 1) // 2
    mine, other = list(panels), None
    pieces = [[] for _ in panels]
    fresh = [[] for _ in panels]
    for period in range(steps + 1):
        last = period == steps
        if last and period:
            other[0], extra = lax.optimization_barrier((other[0], extra))
        other = [hop(o) for o in other] if period else [hand_over(p) for p in panels]
        if not period:
            extra = on_first(other[0])
        arrived = [[] for _ in panels]
        if not last or chips % 2 == 0:
            mine = [hop(m) for m in mine]
            arrived = [[m] for m in mine]
        for i, o in enumerate(other):
            pieces[i] += [(a, 0, rows) for a in [o] + arrived[i]]
            fresh[i] += [o] + arrived[i]
        if last:
            for i in range(len(panels)):
                if fresh[i]:
                    block = jnp.concatenate(fresh[i], axis=0)
                    if i == 0:
                        now = [k for k, piece in enumerate(pieces[0]) if k and piece[0].shape[0] == rows]
                        late = [k for k in range(1, len(pieces[0]) + 1) if k not in now]
                        total = on_next([pieces[0][k] for k in now])
                        block, total = lax.optimization_barrier((block, total))
                    block = hand_over(block)
                    pieces[i].append((block, 0, block.shape[0]))
        elif period and period < steps - 1:
            block, at = hand_over(jnp.concatenate([f for g in fresh for f in g], axis=0)), 0
            for i in range(len(panels)):
                upto = at + rows * len(fresh[i])
                pieces[i].append((block, at, upto))
                fresh[i], at = [], upto
    return pieces, (extra, total), late


def row_groups(rows, step):
    return [slice(r, min(r + step, rows)) for r in range(0, rows, step)]


def panel_groups(refs, spans):
    groups, at = [], 0
    for ref, (low, high) in zip(refs, spans):
        for rows in row_groups(high - low, GROUP):
            size = rows.stop - rows.start
            groups.append((ref, slice(low + rows.start, low + rows.stop), slice(at, at + size)))
            at += size
    return groups


def center(rows, mean):
    return (rows.astype(jnp.float32) - mean).astype(jnp.bfloat16)


def center_group(group, cols, mean, centered, squares, first):
    ref, rows, here = group
    part = center(ref[rows, cols], mean[:, cols])
    centered[here, cols] = part
    wide = jnp.square(part.astype(jnp.float32))
    total = wide[:, :LANES]
    for lane in range(LANES, wide.shape[1], LANES):
        total += wide[:, lane : lane + LANES]
    squares[here, :] = total if first else squares[here, :] + total


def add_products(cols, queries, probes, centered, scores, first):
    products = lax.dot_general(
        centered[:, cols], probes[cols, queries], (((1,), (0,)), ((), ())),
        preferred_element_type=jnp.float32,
    )
    scores[:, queries] = products if first else scores[:, queries] + products


def interleave(features, prepare, probes, centered, scores):
    waiting = []
    for start in range(0, features, CHUNK):
        cols, first = slice(start, start + CHUNK), start == 0
        work = prepare(cols, first)
        share = -(-len(work) // max(len(waiting), 1))
        for i in range(0, len(work), share):
            if waiting:
                waiting.pop(0)()
            for step in work[i : i + share]:
                step()
        waiting += [
            functools.partial(add_products, cols, queries, probes, centered, scores, first)
            for queries in row_groups(probes.shape[1], BLOCK)
        ]
    for step in waiting:
        step()


def log_sum(squares, scores, queries):
    half = 0.5 * jnp.sum(squares[...], axis=1, keepdims=True)
    x = (scores[:, queries] - half) * (1 / TEMP)
    top = jnp.max(x, axis=0, keepdims=True)
    return jnp.log(jnp.sum(jnp.exp(x - top), axis=0, keepdims=True)) + top


def total_kernel(spans, *refs):
    *panel, total = refs
    for start in range(0, total.shape[1], CHUNK):
        cols = slice(start, start + CHUNK)
        sums = [
            jnp.sum(ref[low:high, cols].astype(jnp.float32), axis=0, keepdims=True)
            for ref, (low, high) in zip(panel, spans)
        ]
        total[:, cols] = functools.reduce(jnp.add, sums)


def feature_total(pieces, cost):
    in_vmem = pl.BlockSpec(memory_space=pltpu.VMEM)
    spans = [(low, high) for _, low, high in pieces]
    arrays = [array for array, _, _ in pieces]
    return pl.pallas_call(
        functools.partial(total_kernel, spans),
        out_shape=jax.ShapeDtypeStruct((1, arrays[0].shape[1]), jnp.float32),
        in_specs=[in_vmem] * len(arrays),
        out_specs=in_vmem,
        compiler_params=pltpu.CompilerParams(vmem_limit_bytes=LIMIT),
        cost_estimate=pl.CostEstimate(flops=0, bytes_accessed=cost, transcendentals=0),
    )(*arrays)


def ref_kernel(late, spans, queries, *refs):
    totals, refs = refs[:2], refs[2:]
    panel, (probes, mean, ref_log, centered, squares, scores) = refs[: len(spans)], refs[len(spans) :]
    groups = panel_groups(panel, spans)
    count, features = centered.shape
    for start in range(0, features, CHUNK):
        cols = slice(start, start + CHUNK)
        total = totals[0][:, cols] + totals[1][:, cols]
        for k in late:
            low, high = spans[k]
            total += jnp.sum(panel[k][low:high, cols].astype(jnp.float32), axis=0, keepdims=True)
        mean[:, cols] = total / count

    def center_queries(rows, cols):
        probes[cols, rows] = center(queries[rows, cols], mean[:, cols]).T

    def prepare(cols, first):
        work = []
        for group in groups:
            work.append(functools.partial(center_group, group, cols, mean, centered, squares, first))
        for rows in row_groups(probes.shape[1], LANES):
            for part in row_groups(CHUNK, TURN):
                part = slice(cols.start + part.start, cols.start + part.stop)
                work.append(functools.partial(center_queries, rows, part))
        return work

    interleave(features, prepare, probes, centered, scores)
    for block in row_groups(probes.shape[1], BLOCK):
        ref_log[:, block] = log_sum(squares, scores, block)


def gen_kernel(spans, ref_log, probes, mean, *refs):
    panel, (proof, centered, squares, scores) = refs[: len(spans)], refs[len(spans) :]
    groups = panel_groups(panel, spans)

    def prepare(cols, first):
        return [
            functools.partial(center_group, group, cols, mean, centered, squares, first)
            for group in groups
        ]

    interleave(centered.shape[1], prepare, probes, centered, scores)
    for block in row_groups(probes.shape[1], BLOCK):
        proof[:, block] = log_sum(squares, scores, block) - ref_log[:, block]


def call(kernel, before, pieces, count, out_shape):
    spans = [(low, high) for _, low, high in pieces]
    operands = [*before, *(array for array, _, _ in pieces)]
    rows, features = sum(high - low for low, high in spans), operands[-1].shape[1]
    in_vmem = pl.BlockSpec(memory_space=pltpu.VMEM)
    return pl.pallas_call(
        functools.partial(kernel, spans),
        out_shape=out_shape,
        in_specs=[in_vmem] * len(operands),
        out_specs=jax.tree.map(lambda _: in_vmem, out_shape),
        scratch_shapes=[
            pltpu.VMEM((rows, features), jnp.bfloat16),
            pltpu.VMEM((rows, LANES), jnp.float32),
            pltpu.VMEM((rows, count), jnp.float32),
        ],
        compiler_params=pltpu.CompilerParams(vmem_limit_bytes=LIMIT),
        cost_estimate=pl.CostEstimate(
            flops=2 * rows * count * features,
            bytes_accessed=2 * (rows + count) * features,
            transcendentals=rows * count,
        ),
    )(*operands)


def body(queries, gen_panel, ref_panel):
    panels = [ref_panel, gen_panel]
    (ref_pieces, gen_pieces), totals, late = gather_panels(
        panels,
        lax.axis_size("samp"),
        lambda rows: feature_total([(rows, 0, rows.shape[0])], 4 * queries.size),
        lambda pieces: feature_total(pieces, 0),
    )
    count, features = queries.shape
    logs = jax.ShapeDtypeStruct((1, count), jnp.float32)
    probes, mean, ref_log = call(
        functools.partial(ref_kernel, late),
        [queries, *totals],
        ref_pieces,
        count,
        (
            jax.ShapeDtypeStruct((features, count), jnp.bfloat16),
            jax.ShapeDtypeStruct((1, features), jnp.float32),
            logs,
        ),
    )
    return call(gen_kernel, [ref_log, probes, mean], gen_pieces, count, logs).reshape(-1)


def solution(mesh):
    return jax.shard_map(
        body,
        mesh=mesh,
        in_specs=(
            P(("groups", "samp"), None),
            P(("groups", "samp"), None),
            P(("groups", "samp"), None),
        ),
        out_specs=P(("groups", "samp")),
        check_vma=False,
    )
```

```python
import functools

import jax
import jax.numpy as jnp
from jax import lax
from jax.experimental import pallas as pl
from jax.experimental.pallas import tpu as pltpu
from jax.sharding import PartitionSpec as P

TEMP = 64
LANES = 128
CHUNK = 2048
GROUP = 32
BLOCK = 256
LIMIT = 40 * 2**20


def ring_of_chips(chips):
    return list(range(0, chips, 2)) + list(range(chips - 1 - chips % 2, 0, -2))


def ring_pairs(size):
    order = ring_of_chips(size // 2)
    pairs = []
    for place, chip in enumerate(order):
        after = order[(place + 1) % len(order)]
        before = order[place - 1]
        pairs.append((2 * chip, 2 * after))
        pairs.append((2 * chip + 1, 2 * before + 1))
    return pairs


def core_pairs(size):
    return [(i, i ^ 1) for i in range(size)]


def gather_panels(panels, size, on_first, on_next):
    twins, ring = core_pairs(size), ring_pairs(size)
    chips, rows = size // 2, panels[0].shape[0]

    def hop(block):
        return lax.ppermute(block, "samp", ring)

    def hand_over(block):
        return lax.ppermute(block, "samp", twins)

    steps = (chips - 1) // 2
    mine, other = list(panels), None
    pieces = [[] for _ in panels]
    fresh = [[] for _ in panels]
    for period in range(steps + 1):
        last = period == steps
        if last and period:
            other[0], extra = lax.optimization_barrier((other[0], extra))
        other = [hop(o) for o in other] if period else [hand_over(p) for p in panels]
        if not period:
            extra = on_first(other[0])
        arrived = [[] for _ in panels]
        if not last or chips % 2 == 0:
            mine = [hop(m) for m in mine]
            arrived = [[m] for m in mine]
        for i, o in enumerate(other):
            pieces[i] += [(a, 0, rows) for a in [o] + arrived[i]]
            fresh[i] += [o] + arrived[i]
        if last:
            for i in range(len(panels)):
                if fresh[i]:
                    block = jnp.concatenate(fresh[i], axis=0)
                    if i == 0:
                        now = [k for k, piece in enumerate(pieces[0]) if k and piece[0].shape[0] == rows]
                        late = [k for k in range(1, len(pieces[0]) + 1) if k not in now]
                        total = on_next([pieces[0][k] for k in now])
                        block, total = lax.optimization_barrier((block, total))
                    block = hand_over(block)
                    pieces[i].append((block, 0, block.shape[0]))
        elif period and period < steps - 1:
            block, at = hand_over(jnp.concatenate([f for g in fresh for f in g], axis=0)), 0
            for i in range(len(panels)):
                upto = at + rows * len(fresh[i])
                pieces[i].append((block, at, upto))
                fresh[i], at = [], upto
    return pieces, (extra, total), late


def row_groups(rows, step):
    return [slice(r, min(r + step, rows)) for r in range(0, rows, step)]


def panel_groups(refs, spans):
    groups, at = [], 0
    for ref, (low, high) in zip(refs, spans):
        for rows in row_groups(high - low, GROUP):
            size = rows.stop - rows.start
            groups.append((ref, slice(low + rows.start, low + rows.stop), slice(at, at + size)))
            at += size
    return groups


def center(rows, mean):
    return (rows.astype(jnp.float32) - mean).astype(jnp.bfloat16)


def center_group(group, cols, mean, centered, squares, first):
    ref, rows, here = group
    part = center(ref[rows, cols], mean[:, cols])
    centered[here, cols] = part
    wide = jnp.square(part.astype(jnp.float32))
    total = wide[:, :LANES]
    for lane in range(LANES, wide.shape[1], LANES):
        total += wide[:, lane : lane + LANES]
    squares[here, :] = total if first else squares[here, :] + total


def add_products(cols, queries, probes, centered, scores, first):
    products = lax.dot_general(
        centered[:, cols], probes[queries, cols], (((1,), (1,)), ((), ())),
        preferred_element_type=jnp.float32,
    )
    scores[:, queries] = products if first else scores[:, queries] + products


def interleave(features, prepare, probes, centered, scores):
    waiting = []
    for start in range(0, features, CHUNK):
        cols, first = slice(start, start + CHUNK), start == 0
        work = prepare(cols, first)
        share = -(-len(work) // max(len(waiting), 1))
        for i in range(0, len(work), share):
            if waiting:
                waiting.pop(0)()
            for step in work[i : i + share]:
                step()
        waiting += [
            functools.partial(add_products, cols, queries, probes, centered, scores, first)
            for queries in row_groups(probes.shape[0], BLOCK)
        ]
    for step in waiting:
        step()


def log_sum(squares, scores, queries):
    half = 0.5 * jnp.sum(squares[...], axis=1, keepdims=True)
    x = (scores[:, queries] - half) * (1 / TEMP)
    top = jnp.max(x, axis=0, keepdims=True)
    return jnp.log(jnp.sum(jnp.exp(x - top), axis=0, keepdims=True)) + top


def total_kernel(spans, *refs):
    *panel, total = refs
    for start in range(0, total.shape[1], CHUNK):
        cols = slice(start, start + CHUNK)
        sums = [
            jnp.sum(ref[low:high, cols].astype(jnp.float32), axis=0, keepdims=True)
            for ref, (low, high) in zip(panel, spans)
        ]
        total[:, cols] = functools.reduce(jnp.add, sums)


def feature_total(pieces, cost):
    in_vmem = pl.BlockSpec(memory_space=pltpu.VMEM)
    spans = [(low, high) for _, low, high in pieces]
    arrays = [array for array, _, _ in pieces]
    return pl.pallas_call(
        functools.partial(total_kernel, spans),
        out_shape=jax.ShapeDtypeStruct((1, arrays[0].shape[1]), jnp.float32),
        in_specs=[in_vmem] * len(arrays),
        out_specs=in_vmem,
        compiler_params=pltpu.CompilerParams(vmem_limit_bytes=LIMIT),
        cost_estimate=pl.CostEstimate(flops=0, bytes_accessed=cost, transcendentals=0),
    )(*arrays)


def ref_kernel(late, spans, queries, *refs):
    totals, refs = refs[:2], refs[2:]
    panel, (probes, mean, ref_log, centered, squares, scores) = refs[: len(spans)], refs[len(spans) :]
    groups = panel_groups(panel, spans)
    count, features = centered.shape
    for start in range(0, features, CHUNK):
        cols = slice(start, start + CHUNK)
        total = totals[0][:, cols] + totals[1][:, cols]
        for k in late:
            low, high = spans[k]
            total += jnp.sum(panel[k][low:high, cols].astype(jnp.float32), axis=0, keepdims=True)
        mean[:, cols] = total / count

    def center_queries(rows, cols):
        probes[rows, cols] = center(queries[rows, cols], mean[:, cols])

    def prepare(cols, first):
        work = []
        for group in groups:
            work.append(functools.partial(center_group, group, cols, mean, centered, squares, first))
        for rows in row_groups(probes.shape[0], GROUP):
            work.append(functools.partial(center_queries, rows, cols))
        return work

    interleave(features, prepare, probes, centered, scores)
    for block in row_groups(probes.shape[0], BLOCK):
        ref_log[:, block] = log_sum(squares, scores, block)


def gen_kernel(spans, ref_log, probes, mean, *refs):
    panel, (proof, centered, squares, scores) = refs[: len(spans)], refs[len(spans) :]
    groups = panel_groups(panel, spans)

    def prepare(cols, first):
        return [
            functools.partial(center_group, group, cols, mean, centered, squares, first)
            for group in groups
        ]

    interleave(centered.shape[1], prepare, probes, centered, scores)
    for block in row_groups(probes.shape[0], BLOCK):
        proof[:, block] = log_sum(squares, scores, block) - ref_log[:, block]


def call(kernel, before, pieces, count, out_shape):
    spans = [(low, high) for _, low, high in pieces]
    operands = [*before, *(array for array, _, _ in pieces)]
    rows, features = sum(high - low for low, high in spans), operands[-1].shape[1]
    in_vmem = pl.BlockSpec(memory_space=pltpu.VMEM)
    return pl.pallas_call(
        functools.partial(kernel, spans),
        out_shape=out_shape,
        in_specs=[in_vmem] * len(operands),
        out_specs=jax.tree.map(lambda _: in_vmem, out_shape),
        scratch_shapes=[
            pltpu.VMEM((rows, features), jnp.bfloat16),
            pltpu.VMEM((rows, LANES), jnp.float32),
            pltpu.VMEM((rows, count), jnp.float32),
        ],
        compiler_params=pltpu.CompilerParams(vmem_limit_bytes=LIMIT),
        cost_estimate=pl.CostEstimate(
            flops=2 * rows * count * features,
            bytes_accessed=2 * (rows + count) * features,
            transcendentals=rows * count,
        ),
    )(*operands)


def body(queries, gen_panel, ref_panel):
    panels = [ref_panel, gen_panel]
    (ref_pieces, gen_pieces), totals, late = gather_panels(
        panels,
        lax.axis_size("samp"),
        lambda rows: feature_total([(rows, 0, rows.shape[0])], 4 * queries.size),
        lambda pieces: feature_total(pieces, 0),
    )
    count, features = queries.shape
    logs = jax.ShapeDtypeStruct((1, count), jnp.float32)
    probes, mean, ref_log = call(
        functools.partial(ref_kernel, late),
        [queries, *totals],
        ref_pieces,
        count,
        (
            jax.ShapeDtypeStruct((count, features), jnp.bfloat16),
            jax.ShapeDtypeStruct((1, features), jnp.float32),
            logs,
        ),
    )
    return call(gen_kernel, [ref_log, probes, mean], gen_pieces, count, logs).reshape(-1)


def solution(mesh):
    return jax.shard_map(
        body,
        mesh=mesh,
        in_specs=(
            P(("groups", "samp"), None),
            P(("groups", "samp"), None),
            P(("groups", "samp"), None),
        ),
        out_specs=P(("groups", "samp")),
        check_vma=False,
    )
```

```python
import functools

import jax
import jax.numpy as jnp
from jax import lax
from jax.experimental import pallas as pl
from jax.experimental.pallas import tpu as pltpu
from jax.sharding import PartitionSpec as P

TEMP = 64
LANES = 128
CHUNK = 1024
GROUP = 32
BLOCK = 256
LIMIT = 40 * 2**20


def ring_of_chips(chips):
    return list(range(0, chips, 2)) + list(range(chips - 1 - chips % 2, 0, -2))


def ring_pairs(size):
    order = ring_of_chips(size // 2)
    pairs = []
    for place, chip in enumerate(order):
        after = order[(place + 1) % len(order)]
        before = order[place - 1]
        pairs.append((2 * chip, 2 * after))
        pairs.append((2 * chip + 1, 2 * before + 1))
    return pairs


def core_pairs(size):
    return [(i, i ^ 1) for i in range(size)]


def gather_panels(panels, size, on_first, on_next):
    twins, ring = core_pairs(size), ring_pairs(size)
    chips, rows = size // 2, panels[0].shape[0]

    def hop(block):
        return lax.ppermute(block, "samp", ring)

    def hand_over(block):
        return lax.ppermute(block, "samp", twins)

    steps = (chips - 1) // 2
    mine, other = list(panels), None
    pieces = [[] for _ in panels]
    fresh = [[] for _ in panels]
    for period in range(steps + 1):
        last = period == steps
        if last and period:
            other[0], extra = lax.optimization_barrier((other[0], extra))
        other = [hop(o) for o in other] if period else [hand_over(p) for p in panels]
        if not period:
            extra = on_first(other[0])
        arrived = [[] for _ in panels]
        if not last or chips % 2 == 0:
            mine = [hop(m) for m in mine]
            arrived = [[m] for m in mine]
        for i, o in enumerate(other):
            pieces[i] += [(a, 0, rows) for a in [o] + arrived[i]]
            fresh[i] += [o] + arrived[i]
        if last:
            for i in range(len(panels)):
                if fresh[i]:
                    block = jnp.concatenate(fresh[i], axis=0)
                    if i == 0:
                        now = [k for k, piece in enumerate(pieces[0]) if k and piece[0].shape[0] == rows]
                        late = [k for k in range(1, len(pieces[0]) + 1) if k not in now]
                        total = on_next([pieces[0][k] for k in now])
                        block, total = lax.optimization_barrier((block, total))
                    block = hand_over(block)
                    pieces[i].append((block, 0, block.shape[0]))
        elif period and period < steps - 1:
            block, at = hand_over(jnp.concatenate([f for g in fresh for f in g], axis=0)), 0
            for i in range(len(panels)):
                upto = at + rows * len(fresh[i])
                pieces[i].append((block, at, upto))
                fresh[i], at = [], upto
    return pieces, (extra, total), late


def row_groups(rows, step):
    return [slice(r, min(r + step, rows)) for r in range(0, rows, step)]


def panel_groups(refs, spans):
    groups, at = [], 0
    for ref, (low, high) in zip(refs, spans):
        for rows in row_groups(high - low, GROUP):
            size = rows.stop - rows.start
            groups.append((ref, slice(low + rows.start, low + rows.stop), slice(at, at + size)))
            at += size
    return groups


def center(rows, mean):
    return (rows.astype(jnp.float32) - mean).astype(jnp.bfloat16)


def center_group(group, cols, mean, centered, squares, first):
    ref, rows, here = group
    part = center(ref[rows, cols], mean[:, cols])
    centered[here, cols] = part
    wide = jnp.square(part.astype(jnp.float32))
    total = wide[:, :LANES]
    for lane in range(LANES, wide.shape[1], LANES):
        total += wide[:, lane : lane + LANES]
    squares[here, :] = total if first else squares[here, :] + total


def add_products(cols, queries, probes, centered, scores, first):
    products = lax.dot_general(
        centered[:, cols], probes[queries, cols], (((1,), (1,)), ((), ())),
        preferred_element_type=jnp.float32,
    )
    scores[:, queries] = products if first else scores[:, queries] + products


def interleave(features, prepare, probes, centered, scores):
    waiting = []
    for start in range(0, features, CHUNK):
        cols, first = slice(start, start + CHUNK), start == 0
        work = prepare(cols, first)
        share = -(-len(work) // max(len(waiting), 1))
        for i in range(0, len(work), share):
            if waiting:
                waiting.pop(0)()
            for step in work[i : i + share]:
                step()
        waiting += [
            functools.partial(add_products, cols, queries, probes, centered, scores, first)
            for queries in row_groups(probes.shape[0], BLOCK)
        ]
    for step in waiting:
        step()


def log_sum(squares, scores, queries):
    half = 0.5 * jnp.sum(squares[...], axis=1, keepdims=True)
    x = (scores[:, queries] - half) * (1 / TEMP)
    top = jnp.max(x, axis=0, keepdims=True)
    return jnp.log(jnp.sum(jnp.exp(x - top), axis=0, keepdims=True)) + top


def total_kernel(spans, *refs):
    *panel, total = refs
    for start in range(0, total.shape[1], CHUNK):
        cols = slice(start, start + CHUNK)
        sums = [
            jnp.sum(ref[low:high, cols].astype(jnp.float32), axis=0, keepdims=True)
            for ref, (low, high) in zip(panel, spans)
        ]
        total[:, cols] = functools.reduce(jnp.add, sums)


def feature_total(pieces, cost):
    in_vmem = pl.BlockSpec(memory_space=pltpu.VMEM)
    spans = [(low, high) for _, low, high in pieces]
    arrays = [array for array, _, _ in pieces]
    return pl.pallas_call(
        functools.partial(total_kernel, spans),
        out_shape=jax.ShapeDtypeStruct((1, arrays[0].shape[1]), jnp.float32),
        in_specs=[in_vmem] * len(arrays),
        out_specs=in_vmem,
        compiler_params=pltpu.CompilerParams(vmem_limit_bytes=LIMIT),
        cost_estimate=pl.CostEstimate(flops=0, bytes_accessed=cost, transcendentals=0),
    )(*arrays)


def ref_kernel(late, spans, queries, *refs):
    totals, refs = refs[:2], refs[2:]
    panel, (probes, mean, ref_log, centered, squares, scores) = refs[: len(spans)], refs[len(spans) :]
    groups = panel_groups(panel, spans)
    count, features = centered.shape
    def take_mean(cols):
        total = totals[0][:, cols] + totals[1][:, cols]
        for k in late:
            low, high = spans[k]
            total += jnp.sum(panel[k][low:high, cols].astype(jnp.float32), axis=0, keepdims=True)
        mean[:, cols] = total / count

    def center_queries(rows, cols):
        probes[rows, cols] = center(queries[rows, cols], mean[:, cols])

    def prepare(cols, first):
        work = [functools.partial(take_mean, cols)]
        for group in groups:
            work.append(functools.partial(center_group, group, cols, mean, centered, squares, first))
        for rows in row_groups(probes.shape[0], GROUP):
            work.append(functools.partial(center_queries, rows, cols))
        return work

    interleave(features, prepare, probes, centered, scores)
    for block in row_groups(probes.shape[0], BLOCK):
        ref_log[:, block] = log_sum(squares, scores, block)


def gen_kernel(spans, ref_log, probes, mean, *refs):
    panel, (proof, centered, squares, scores) = refs[: len(spans)], refs[len(spans) :]
    groups = panel_groups(panel, spans)

    def prepare(cols, first):
        return [
            functools.partial(center_group, group, cols, mean, centered, squares, first)
            for group in groups
        ]

    interleave(centered.shape[1], prepare, probes, centered, scores)
    for block in row_groups(probes.shape[0], BLOCK):
        proof[:, block] = log_sum(squares, scores, block) - ref_log[:, block]


def call(kernel, before, pieces, count, out_shape):
    spans = [(low, high) for _, low, high in pieces]
    operands = [*before, *(array for array, _, _ in pieces)]
    rows, features = sum(high - low for low, high in spans), operands[-1].shape[1]
    in_vmem = pl.BlockSpec(memory_space=pltpu.VMEM)
    return pl.pallas_call(
        functools.partial(kernel, spans),
        out_shape=out_shape,
        in_specs=[in_vmem] * len(operands),
        out_specs=jax.tree.map(lambda _: in_vmem, out_shape),
        scratch_shapes=[
            pltpu.VMEM((rows, features), jnp.bfloat16),
            pltpu.VMEM((rows, LANES), jnp.float32),
            pltpu.VMEM((rows, count), jnp.float32),
        ],
        compiler_params=pltpu.CompilerParams(vmem_limit_bytes=LIMIT),
        cost_estimate=pl.CostEstimate(
            flops=2 * rows * count * features,
            bytes_accessed=2 * (rows + count) * features,
            transcendentals=rows * count,
        ),
    )(*operands)


def body(queries, gen_panel, ref_panel):
    panels = [ref_panel, gen_panel]
    (ref_pieces, gen_pieces), totals, late = gather_panels(
        panels,
        lax.axis_size("samp"),
        lambda rows: feature_total([(rows, 0, rows.shape[0])], 4 * queries.size),
        lambda pieces: feature_total(pieces, 0),
    )
    count, features = queries.shape
    logs = jax.ShapeDtypeStruct((1, count), jnp.float32)
    probes, mean, ref_log = call(
        functools.partial(ref_kernel, late),
        [queries, *totals],
        ref_pieces,
        count,
        (
            jax.ShapeDtypeStruct((count, features), jnp.bfloat16),
            jax.ShapeDtypeStruct((1, features), jnp.float32),
            logs,
        ),
    )
    return call(gen_kernel, [ref_log, probes, mean], gen_pieces, count, logs).reshape(-1)


def solution(mesh):
    return jax.shard_map(
        body,
        mesh=mesh,
        in_specs=(
            P(("groups", "samp"), None),
            P(("groups", "samp"), None),
            P(("groups", "samp"), None),
        ),
        out_specs=P(("groups", "samp")),
        check_vma=False,
    )
```

```python
import functools

import jax
import jax.numpy as jnp
from jax import lax
from jax.experimental import pallas as pl
from jax.experimental.pallas import tpu as pltpu
from jax.sharding import PartitionSpec as P

TEMP = 64
LANES = 128
CHUNK = 1024
GROUP = 32
BLOCK = 512
LIMIT = 40 * 2**20


def ring_of_chips(chips):
    return list(range(0, chips, 2)) + list(range(chips - 1 - chips % 2, 0, -2))


def ring_pairs(size):
    order = ring_of_chips(size // 2)
    pairs = []
    for place, chip in enumerate(order):
        after = order[(place + 1) % len(order)]
        before = order[place - 1]
        pairs.append((2 * chip, 2 * after))
        pairs.append((2 * chip + 1, 2 * before + 1))
    return pairs


def core_pairs(size):
    return [(i, i ^ 1) for i in range(size)]


def gather_panels(panels, size, on_first, on_next):
    twins, ring = core_pairs(size), ring_pairs(size)
    chips, rows = size // 2, panels[0].shape[0]

    def hop(block):
        return lax.ppermute(block, "samp", ring)

    def hand_over(block):
        return lax.ppermute(block, "samp", twins)

    steps = (chips - 1) // 2
    mine, other = list(panels), None
    pieces = [[] for _ in panels]
    fresh = [[] for _ in panels]
    for period in range(steps + 1):
        last = period == steps
        if last and period:
            other[0], extra = lax.optimization_barrier((other[0], extra))
        other = [hop(o) for o in other] if period else [hand_over(p) for p in panels]
        if not period:
            extra = on_first(other[0])
        arrived = [[] for _ in panels]
        if not last or chips % 2 == 0:
            mine = [hop(m) for m in mine]
            arrived = [[m] for m in mine]
        for i, o in enumerate(other):
            pieces[i] += [(a, 0, rows) for a in [o] + arrived[i]]
            fresh[i] += [o] + arrived[i]
        if last:
            for i in range(len(panels)):
                if fresh[i]:
                    block = jnp.concatenate(fresh[i], axis=0)
                    if i == 0:
                        now = [k for k, piece in enumerate(pieces[0]) if k and piece[0].shape[0] == rows]
                        late = [k for k in range(1, len(pieces[0]) + 1) if k not in now]
                        total = on_next([pieces[0][k] for k in now])
                        block, total = lax.optimization_barrier((block, total))
                    block = hand_over(block)
                    pieces[i].append((block, 0, block.shape[0]))
        elif period and period < steps - 1:
            block, at = hand_over(jnp.concatenate([f for g in fresh for f in g], axis=0)), 0
            for i in range(len(panels)):
                upto = at + rows * len(fresh[i])
                pieces[i].append((block, at, upto))
                fresh[i], at = [], upto
    return pieces, (extra, total), late


def row_groups(rows, step):
    return [slice(r, min(r + step, rows)) for r in range(0, rows, step)]


def panel_groups(refs, spans):
    groups, at = [], 0
    for ref, (low, high) in zip(refs, spans):
        for rows in row_groups(high - low, GROUP):
            size = rows.stop - rows.start
            groups.append((ref, slice(low + rows.start, low + rows.stop), slice(at, at + size)))
            at += size
    return groups


def center(rows, mean):
    return (rows.astype(jnp.float32) - mean).astype(jnp.bfloat16)


def center_group(group, cols, mean, centered, squares, first):
    ref, rows, here = group
    part = center(ref[rows, cols], mean[:, cols])
    centered[here, cols] = part
    wide = jnp.square(part.astype(jnp.float32))
    total = wide[:, :LANES]
    for lane in range(LANES, wide.shape[1], LANES):
        total += wide[:, lane : lane + LANES]
    squares[here, :] = total if first else squares[here, :] + total


def add_products(cols, queries, probes, centered, scores, first):
    products = lax.dot_general(
        centered[:, cols], probes[queries, cols], (((1,), (1,)), ((), ())),
        preferred_element_type=jnp.float32,
    )
    scores[:, queries] = products if first else scores[:, queries] + products


def interleave(features, prepare, probes, centered, scores):
    waiting = []
    for start in range(0, features, CHUNK):
        cols, first = slice(start, start + CHUNK), start == 0
        work = prepare(cols, first)
        share = -(-len(work) // max(len(waiting), 1))
        for i in range(0, len(work), share):
            if waiting:
                waiting.pop(0)()
            for step in work[i : i + share]:
                step()
        waiting += [
            functools.partial(add_products, cols, queries, probes, centered, scores, first)
            for queries in row_groups(probes.shape[0], BLOCK)
        ]
    for step in waiting:
        step()


def log_sum(squares, scores, queries):
    half = 0.5 * jnp.sum(squares[...], axis=1, keepdims=True)
    x = (scores[:, queries] - half) * (1 / TEMP)
    top = jnp.max(x, axis=0, keepdims=True)
    return jnp.log(jnp.sum(jnp.exp(x - top), axis=0, keepdims=True)) + top


def total_kernel(spans, *refs):
    *panel, total = refs
    for start in range(0, total.shape[1], CHUNK):
        cols = slice(start, start + CHUNK)
        sums = [
            jnp.sum(ref[low:high, cols].astype(jnp.float32), axis=0, keepdims=True)
            for ref, (low, high) in zip(panel, spans)
        ]
        total[:, cols] = functools.reduce(jnp.add, sums)


def feature_total(pieces, cost):
    in_vmem = pl.BlockSpec(memory_space=pltpu.VMEM)
    spans = [(low, high) for _, low, high in pieces]
    arrays = [array for array, _, _ in pieces]
    return pl.pallas_call(
        functools.partial(total_kernel, spans),
        out_shape=jax.ShapeDtypeStruct((1, arrays[0].shape[1]), jnp.float32),
        in_specs=[in_vmem] * len(arrays),
        out_specs=in_vmem,
        compiler_params=pltpu.CompilerParams(vmem_limit_bytes=LIMIT),
        cost_estimate=pl.CostEstimate(flops=0, bytes_accessed=cost, transcendentals=0),
    )(*arrays)


def ref_kernel(late, spans, queries, *refs):
    totals, refs = refs[:2], refs[2:]
    panel, (probes, mean, ref_log, centered, squares, scores) = refs[: len(spans)], refs[len(spans) :]
    groups = panel_groups(panel, spans)
    count, features = centered.shape
    for start in range(0, features, CHUNK):
        cols = slice(start, start + CHUNK)
        total = totals[0][:, cols] + totals[1][:, cols]
        for k in late:
            low, high = spans[k]
            total += jnp.sum(panel[k][low:high, cols].astype(jnp.float32), axis=0, keepdims=True)
        mean[:, cols] = total / count

    def center_queries(rows, cols):
        probes[rows, cols] = center(queries[rows, cols], mean[:, cols])

    def prepare(cols, first):
        work = []
        for group in groups:
            work.append(functools.partial(center_group, group, cols, mean, centered, squares, first))
        for rows in row_groups(probes.shape[0], GROUP):
            work.append(functools.partial(center_queries, rows, cols))
        return work

    interleave(features, prepare, probes, centered, scores)
    for block in row_groups(probes.shape[0], BLOCK):
        ref_log[:, block] = log_sum(squares, scores, block)


def gen_kernel(spans, ref_log, probes, mean, *refs):
    panel, (proof, centered, squares, scores) = refs[: len(spans)], refs[len(spans) :]
    groups = panel_groups(panel, spans)

    def prepare(cols, first):
        return [
            functools.partial(center_group, group, cols, mean, centered, squares, first)
            for group in groups
        ]

    interleave(centered.shape[1], prepare, probes, centered, scores)
    for block in row_groups(probes.shape[0], BLOCK):
        proof[:, block] = log_sum(squares, scores, block) - ref_log[:, block]


def call(kernel, before, pieces, count, out_shape):
    spans = [(low, high) for _, low, high in pieces]
    operands = [*before, *(array for array, _, _ in pieces)]
    rows, features = sum(high - low for low, high in spans), operands[-1].shape[1]
    in_vmem = pl.BlockSpec(memory_space=pltpu.VMEM)
    return pl.pallas_call(
        functools.partial(kernel, spans),
        out_shape=out_shape,
        in_specs=[in_vmem] * len(operands),
        out_specs=jax.tree.map(lambda _: in_vmem, out_shape),
        scratch_shapes=[
            pltpu.VMEM((rows, features), jnp.bfloat16),
            pltpu.VMEM((rows, LANES), jnp.float32),
            pltpu.VMEM((rows, count), jnp.float32),
        ],
        compiler_params=pltpu.CompilerParams(vmem_limit_bytes=LIMIT),
        cost_estimate=pl.CostEstimate(
            flops=2 * rows * count * features,
            bytes_accessed=2 * (rows + count) * features,
            transcendentals=rows * count,
        ),
    )(*operands)


def body(queries, gen_panel, ref_panel):
    panels = [ref_panel, gen_panel]
    (ref_pieces, gen_pieces), totals, late = gather_panels(
        panels,
        lax.axis_size("samp"),
        lambda rows: feature_total([(rows, 0, rows.shape[0])], 4 * queries.size),
        lambda pieces: feature_total(pieces, 0),
    )
    count, features = queries.shape
    logs = jax.ShapeDtypeStruct((1, count), jnp.float32)
    probes, mean, ref_log = call(
        functools.partial(ref_kernel, late),
        [queries, *totals],
        ref_pieces,
        count,
        (
            jax.ShapeDtypeStruct((count, features), jnp.bfloat16),
            jax.ShapeDtypeStruct((1, features), jnp.float32),
            logs,
        ),
    )
    return call(gen_kernel, [ref_log, probes, mean], gen_pieces, count, logs).reshape(-1)


def solution(mesh):
    return jax.shard_map(
        body,
        mesh=mesh,
        in_specs=(
            P(("groups", "samp"), None),
            P(("groups", "samp"), None),
            P(("groups", "samp"), None),
        ),
        out_specs=P(("groups", "samp")),
        check_vma=False,
    )
```

```python
import functools

import jax
import jax.numpy as jnp
from jax import lax
from jax.experimental import pallas as pl
from jax.experimental.pallas import tpu as pltpu
from jax.sharding import PartitionSpec as P

TEMP = 64
LANES = 128
CHUNK = 1024
GROUP = 32
BLOCK = 256
LIMIT = 40 * 2**20


def ring_of_chips(chips):
    return list(range(0, chips, 2)) + list(range(chips - 1 - chips % 2, 0, -2))


def ring_pairs(size):
    order = ring_of_chips(size // 2)
    pairs = []
    for place, chip in enumerate(order):
        after = order[(place + 1) % len(order)]
        before = order[place - 1]
        pairs.append((2 * chip, 2 * before))
        pairs.append((2 * chip + 1, 2 * after + 1))
    return pairs


def core_pairs(size):
    return [(i, i ^ 1) for i in range(size)]


def gather_panels(panels, size, on_first, on_next):
    twins, ring = core_pairs(size), ring_pairs(size)
    chips, rows = size // 2, panels[0].shape[0]

    def hop(block):
        return lax.ppermute(block, "samp", ring)

    def hand_over(block):
        return lax.ppermute(block, "samp", twins)

    steps = (chips - 1) // 2
    mine, other = list(panels), None
    pieces = [[] for _ in panels]
    fresh = [[] for _ in panels]
    for period in range(steps + 1):
        last = period == steps
        if last and period:
            other[0], extra = lax.optimization_barrier((other[0], extra))
        other = [hop(o) for o in other] if period else [hand_over(p) for p in panels]
        if not period:
            extra = on_first(other[0])
        arrived = [[] for _ in panels]
        if not last or chips % 2 == 0:
            mine = [hop(m) for m in mine]
            arrived = [[m] for m in mine]
        for i, o in enumerate(other):
            pieces[i] += [(a, 0, rows) for a in [o] + arrived[i]]
            fresh[i] += [o] + arrived[i]
        if last:
            for i in range(len(panels)):
                if fresh[i]:
                    block = jnp.concatenate(fresh[i], axis=0)
                    if i == 0:
                        now = [k for k, piece in enumerate(pieces[0]) if k and piece[0].shape[0] == rows]
                        late = [k for k in range(1, len(pieces[0]) + 1) if k not in now]
                        total = on_next([pieces[0][k] for k in now])
                        block, total = lax.optimization_barrier((block, total))
                    block = hand_over(block)
                    pieces[i].append((block, 0, block.shape[0]))
        elif period and period < steps - 1:
            block, at = hand_over(jnp.concatenate([f for g in fresh for f in g], axis=0)), 0
            for i in range(len(panels)):
                upto = at + rows * len(fresh[i])
                pieces[i].append((block, at, upto))
                fresh[i], at = [], upto
    return pieces, (extra, total), late


def row_groups(rows, step):
    return [slice(r, min(r + step, rows)) for r in range(0, rows, step)]


def panel_groups(refs, spans):
    groups, at = [], 0
    for ref, (low, high) in zip(refs, spans):
        for rows in row_groups(high - low, GROUP):
            size = rows.stop - rows.start
            groups.append((ref, slice(low + rows.start, low + rows.stop), slice(at, at + size)))
            at += size
    return groups


def center(rows, mean):
    return (rows.astype(jnp.float32) - mean).astype(jnp.bfloat16)


def center_group(group, cols, mean, centered, squares, first):
    ref, rows, here = group
    part = center(ref[rows, cols], mean[:, cols])
    centered[here, cols] = part
    wide = jnp.square(part.astype(jnp.float32))
    total = wide[:, :LANES]
    for lane in range(LANES, wide.shape[1], LANES):
        total += wide[:, lane : lane + LANES]
    squares[here, :] = total if first else squares[here, :] + total


def add_products(cols, queries, probes, centered, scores, first):
    products = lax.dot_general(
        centered[:, cols], probes[queries, cols], (((1,), (1,)), ((), ())),
        preferred_element_type=jnp.float32,
    )
    scores[:, queries] = products if first else scores[:, queries] + products


def interleave(features, prepare, probes, centered, scores):
    waiting = []
    for start in range(0, features, CHUNK):
        cols, first = slice(start, start + CHUNK), start == 0
        work = prepare(cols, first)
        share = -(-len(work) // max(len(waiting), 1))
        for i in range(0, len(work), share):
            if waiting:
                waiting.pop(0)()
            for step in work[i : i + share]:
                step()
        waiting += [
            functools.partial(add_products, cols, queries, probes, centered, scores, first)
            for queries in row_groups(probes.shape[0], BLOCK)
        ]
    for step in waiting:
        step()


def log_sum(squares, scores, queries):
    half = 0.5 * jnp.sum(squares[...], axis=1, keepdims=True)
    x = (scores[:, queries] - half) * (1 / TEMP)
    top = jnp.max(x, axis=0, keepdims=True)
    return jnp.log(jnp.sum(jnp.exp(x - top), axis=0, keepdims=True)) + top


def total_kernel(spans, *refs):
    *panel, total = refs
    for start in range(0, total.shape[1], CHUNK):
        cols = slice(start, start + CHUNK)
        sums = [
            jnp.sum(ref[low:high, cols].astype(jnp.float32), axis=0, keepdims=True)
            for ref, (low, high) in zip(panel, spans)
        ]
        total[:, cols] = functools.reduce(jnp.add, sums)


def feature_total(pieces, cost):
    in_vmem = pl.BlockSpec(memory_space=pltpu.VMEM)
    spans = [(low, high) for _, low, high in pieces]
    arrays = [array for array, _, _ in pieces]
    return pl.pallas_call(
        functools.partial(total_kernel, spans),
        out_shape=jax.ShapeDtypeStruct((1, arrays[0].shape[1]), jnp.float32),
        in_specs=[in_vmem] * len(arrays),
        out_specs=in_vmem,
        compiler_params=pltpu.CompilerParams(vmem_limit_bytes=LIMIT),
        cost_estimate=pl.CostEstimate(flops=0, bytes_accessed=cost, transcendentals=0),
    )(*arrays)


def ref_kernel(late, spans, queries, *refs):
    totals, refs = refs[:2], refs[2:]
    panel, (probes, mean, ref_log, centered, squares, scores) = refs[: len(spans)], refs[len(spans) :]
    groups = panel_groups(panel, spans)
    count, features = centered.shape
    for start in range(0, features, CHUNK):
        cols = slice(start, start + CHUNK)
        total = totals[0][:, cols] + totals[1][:, cols]
        for k in late:
            low, high = spans[k]
            total += jnp.sum(panel[k][low:high, cols].astype(jnp.float32), axis=0, keepdims=True)
        mean[:, cols] = total / count

    def center_queries(rows, cols):
        probes[rows, cols] = center(queries[rows, cols], mean[:, cols])

    def prepare(cols, first):
        work = []
        for group in groups:
            work.append(functools.partial(center_group, group, cols, mean, centered, squares, first))
        for rows in row_groups(probes.shape[0], GROUP):
            work.append(functools.partial(center_queries, rows, cols))
        return work

    interleave(features, prepare, probes, centered, scores)
    for block in row_groups(probes.shape[0], BLOCK):
        ref_log[:, block] = log_sum(squares, scores, block)


def gen_kernel(spans, ref_log, probes, mean, *refs):
    panel, (proof, centered, squares, scores) = refs[: len(spans)], refs[len(spans) :]
    groups = panel_groups(panel, spans)

    def prepare(cols, first):
        return [
            functools.partial(center_group, group, cols, mean, centered, squares, first)
            for group in groups
        ]

    interleave(centered.shape[1], prepare, probes, centered, scores)
    for block in row_groups(probes.shape[0], BLOCK):
        proof[:, block] = log_sum(squares, scores, block) - ref_log[:, block]


def call(kernel, before, pieces, count, out_shape):
    spans = [(low, high) for _, low, high in pieces]
    operands = [*before, *(array for array, _, _ in pieces)]
    rows, features = sum(high - low for low, high in spans), operands[-1].shape[1]
    in_vmem = pl.BlockSpec(memory_space=pltpu.VMEM)
    return pl.pallas_call(
        functools.partial(kernel, spans),
        out_shape=out_shape,
        in_specs=[in_vmem] * len(operands),
        out_specs=jax.tree.map(lambda _: in_vmem, out_shape),
        scratch_shapes=[
            pltpu.VMEM((rows, features), jnp.bfloat16),
            pltpu.VMEM((rows, LANES), jnp.float32),
            pltpu.VMEM((rows, count), jnp.float32),
        ],
        compiler_params=pltpu.CompilerParams(vmem_limit_bytes=LIMIT),
        cost_estimate=pl.CostEstimate(
            flops=2 * rows * count * features,
            bytes_accessed=2 * (rows + count) * features,
            transcendentals=rows * count,
        ),
    )(*operands)


def body(queries, gen_panel, ref_panel):
    panels = [ref_panel, gen_panel]
    (ref_pieces, gen_pieces), totals, late = gather_panels(
        panels,
        lax.axis_size("samp"),
        lambda rows: feature_total([(rows, 0, rows.shape[0])], 4 * queries.size),
        lambda pieces: feature_total(pieces, 0),
    )
    count, features = queries.shape
    logs = jax.ShapeDtypeStruct((1, count), jnp.float32)
    probes, mean, ref_log = call(
        functools.partial(ref_kernel, late),
        [queries, *totals],
        ref_pieces,
        count,
        (
            jax.ShapeDtypeStruct((count, features), jnp.bfloat16),
            jax.ShapeDtypeStruct((1, features), jnp.float32),
            logs,
        ),
    )
    return call(gen_kernel, [ref_log, probes, mean], gen_pieces, count, logs).reshape(-1)


def solution(mesh):
    return jax.shard_map(
        body,
        mesh=mesh,
        in_specs=(
            P(("groups", "samp"), None),
            P(("groups", "samp"), None),
            P(("groups", "samp"), None),
        ),
        out_specs=P(("groups", "samp")),
        check_vma=False,
    )
```
